512 devices in a mesh: group: 64 (over x, z_hi, y), slab: 8 (over z_lo, core).
Axes of the slice: x: 4, y: 4, z: 16 (z_hi: 4, z_lo: 4; z = z_hi * 4 + z_lo), core: 2. Of those that a mesh axis runs over, the one named last changes fastest.
Arguments:
- tokens: bfloat16 [64, 1024, 1024], P('group', 'slab'), may hold values from -6 to 6
- norm_gain: float32 [1024], replicated, may hold values from 0.1 to 1.9
- w_qkv: bfloat16 [1024, 3, 1024], P(None, None, 'slab'), may hold values from -0.1875 to 0.1875
- q_gain: float32 [64], replicated, may hold values from 0.5 to 3
- k_gain: float32 [64], replicated, may hold values from 0.5 to 3
- w_out: bfloat16 [1024, 1024], P('slab'), may hold values from -0.1875 to 0.1875
- covis_mask: int32 [64, 64], replicated, may hold values from 0 to 1, as said below
- capture_rank: int32 [64], replicated, may hold values from 0 to 63, each once
Outputs:
- mixed_rows: bfloat16 [64, 1024, 1024], P('group', 'slab')
The draws below stay inside these ranges and needn't reach their ends.
Inputs may be any that keep to these rules, and one draw needn't show every extreme that they name: covis_mask[i, j] is 1 where i = j, 0 where |i - j| > 3, and covis_mask[i, j] = covis_mask[j, i]. `capture_rank`: a permutation of the image numbers.
All inputs are finite; a program needn't handle non-finite values.
Results may differ from the reference program's by a relative error of at most 0.015.
The reference program's roundings to bfloat16 on the way (of `normed`, `weights` and `attended`) count: a program that leaves them out, or rounds other values in their place, can miss the bound.
Values may be sent and summed in bfloat16 or wider, within the bound.
A program may use at most 64 MiB of HBM per device.

```python
import math
import jax
import jax.numpy as jnp
from jax import lax

D = 1024
HEADS = 16
HD = 64
TOK_IMG = 1024
REACH = 3
IMAGES = 64


def draw_covis_mask(key, part):
    coin_flip = jax.random.randint(key, (IMAGES, IMAGES), 0, 5)
    row_index = lax.broadcasted_iota(jnp.int32, (IMAGES, IMAGES), 0)
    col_index = lax.broadcasted_iota(jnp.int32, (IMAGES, IMAGES), 1)
    mirrored = jnp.where(row_index < col_index, coin_flip, jnp.transpose(coin_flip))
    in_band = jnp.abs(row_index - col_index) <= REACH
    linked = (mirrored < 3) & in_band | (row_index == col_index)
    return linked.astype(jnp.int32)


def steps_of(own_key, extent, cuts, least, largest):
    factor_of, own = 1.0, jax.random.fold_in(own_key, 6)
    for position, parts in cuts:
        heights = jnp.exp(jax.random.uniform(jax.random.fold_in(own, position), (parts,), jnp.float32, least / len(cuts), largest / len(cuts)))
        factor_of = factor_of * jnp.repeat(heights, extent[position] // parts).reshape([-1 if axis == position else 1 for axis in range(len(extent))])
    return factor_of


def bell_draw(stream_key, shape, scale, most, cuts=(), kind=jnp.bfloat16):
    result = jax.random.normal(stream_key, shape, jnp.float32) * scale
    if len(cuts) > 0:
        result = steps_of(stream_key, shape, cuts, -0.22, 0.18) * result
    return jnp.clip(result, min=-most, max=most).astype(kind)


def setup_inputs(seed: int = 0) -> dict:
    seeds = jax.random.split(jax.random.key(seed), 9)
    return {
        "tokens": bell_draw(seeds[0], (IMAGES, TOK_IMG, D), 1.0, 6.0, ((0, 64), (1, 8))),
        "norm_gain": jnp.clip(1.0 + 0.18 * jax.random.normal(seeds[1], (D,), jnp.float32), 0.1, 1.9),
        "w_qkv": bell_draw(seeds[2], (D, 3, D), D ** -0.5, 0.1875, ((2, 8),)),
        "q_gain": jnp.clip(jnp.exp(jax.random.uniform(seeds[3], (HD,), jnp.float32, math.log(0.5), math.log(3.0))), 0.5, 3.0),
        "k_gain": jnp.clip(jnp.exp(jax.random.uniform(seeds[4], (HD,), jnp.float32, math.log(0.5), math.log(3.0))), 0.5, 3.0),
        "w_out": bell_draw(seeds[5], (D, D), D ** -0.5, 0.1875, ((0, 8),)),
        "covis_mask": draw_covis_mask(jax.random.fold_in(seeds[8], 71), 0),
        "capture_rank": jax.random.permutation(seeds[7], IMAGES).astype(jnp.int32),
    }


def norm_rows(values, gain):
    centre = lax.optimization_barrier(jnp.mean(values, axis=-1, keepdims=True))
    centred = values - centre
    spread = lax.optimization_barrier(jnp.mean(centred * centred, axis=-1, keepdims=True))
    return centred * lax.rsqrt(spread + 1e-06) * gain

def block_terms(queries, key_rows, values):
    score_scale = HD ** (-0.5)
    scores = jnp.einsum('qhd,khd->hqk', queries.astype(jnp.float32), key_rows.astype(jnp.float32)) * score_scale
    weights = jnp.exp(scores).astype(jnp.bfloat16)
    numerator = jnp.einsum('hqk,khd->qhd', weights.astype(jnp.float32), values.astype(jnp.float32))
    denominator = jnp.transpose(lax.optimization_barrier(jnp.sum(weights.astype(jnp.float32), axis=2)))
    return (numerator, denominator)

def reference(tokens, norm_gain, w_qkv, q_gain, k_gain, w_out, covis_mask, capture_rank):
    flat_w = w_qkv.reshape(D, 3 * D)

    def split_heads(image):
        normed = norm_rows(image.astype(jnp.float32), norm_gain.astype(jnp.float32)).astype(jnp.bfloat16)
        projected = jnp.dot(normed, flat_w, preferred_element_type=jnp.float32).reshape(TOK_IMG, 3, HEADS, HD)
        queries = norm_rows(projected[:, 0], q_gain.astype(jnp.float32)).astype(jnp.bfloat16)
        key_rows = norm_rows(projected[:, 1], k_gain.astype(jnp.float32)).astype(jnp.bfloat16)
        values = projected[:, 2].astype(jnp.bfloat16)
        return (queries, key_rows, values)
    all_queries, all_keys, all_values = lax.map(split_heads, tokens)

    def attend(image_index):
        queries = all_queries[image_index]
        numerator = jnp.zeros((TOK_IMG, HEADS, HD), jnp.float32)
        denominator = jnp.zeros((TOK_IMG, HEADS), jnp.float32)
        for offset in range(-REACH, REACH + 1):
            partner = image_index + offset
            in_range = (partner >= 0) & (partner < IMAGES)
            clipped = jnp.clip(partner, 0, IMAGES - 1).astype(jnp.int32)
            allowed = in_range & (covis_mask[image_index, clipped] == 1) & (capture_rank[clipped] <= capture_rank[image_index])
            key_rows = all_keys[clipped]
            values = all_values[clipped]

            def taken():
                return block_terms(queries, key_rows, values)

            def skipped():
                return (jnp.zeros((TOK_IMG, HEADS, HD), jnp.float32), jnp.zeros((TOK_IMG, HEADS), jnp.float32))
            part_num, part_den = lax.cond(allowed, taken, skipped)
            numerator = numerator + part_num
            denominator = denominator + part_den
        attended = (numerator / denominator[:, :, None]).astype(jnp.bfloat16).reshape(TOK_IMG, D)
        return jnp.dot(attended, w_out, preferred_element_type=jnp.float32).astype(jnp.bfloat16)
    return lax.map(attend, jnp.arange(IMAGES, dtype=jnp.int32))
```

```python
import functools
import math

import jax
import jax.numpy as jnp
from jax import lax
from jax.experimental import pallas as pl
from jax.experimental.pallas import tpu as pltpu
from jax.sharding import PartitionSpec as P

MESH = pl.DeviceIdType.MESH
BF = jnp.bfloat16
F32 = jnp.float32
EPS = 1e-06
EXP_SCALE = 0.125 * math.log2(math.e)


def dot(a, b):
    return jnp.dot(a, b, preferred_element_type=F32)


def kernel(
    tok, ngain, w, qgain, kgain, w_out, covis, rank, out,
    xg, w3, emat, stq, stkv, q_s, kv_s, kvx, acc, wo, fin, fsend,
    loc_sem, ws_sem, ag_send, ag_recv, yq_send, yq_recv, yk_send, yk_recv,
    sib_send, sib_recv, cr_send, cr_recv, cs_send, cs_recv,
    wa_send, wa_recv, wb_send, wb_recv, wc_sem, f_send, f_recv,
):
    g = lax.axis_index("group")
    s = lax.axis_index("slab")
    y = g % 4
    row = g // 4
    base = row * 4
    x = g // 16
    zy = g % 16
    t = s // 2
    c = s % 2
    sib = (g, t * 2 + 1 - c)

    def y_dev(k):
        return (base + (y + k) % 4, s)

    def blk_dev(k, m):
        return (base + (y + k) % 4, ((t + m) % 4) * 2 + c)

    def x_dev(k):
        return (((x + k) % 4) * 16 + zy, s)

    up = ((g + 4) % 64, s)
    down = ((g + 60) % 64, s)

    def rcopy(src, dst, ss, rs, dev):
        return pltpu.make_async_remote_copy(
            src_ref=src, dst_ref=dst, send_sem=ss, recv_sem=rs, device_id=dev, device_id_type=MESH
        )

    barrier = pltpu.get_barrier_semaphore()
    partners = [blk_dev(k, m) for k in range(4) for m in range(4) if k or m]
    partners += [sib, up, down] + [x_dev(k) for k in (1, 2, 3)]
    for dev in partners:
        pl.semaphore_signal(barrier, inc=1, device_id=dev, device_id_type=MESH)

    w_local = pltpu.make_async_copy(w, w3.at[:, :, pl.ds(pl.multiple_of(c * 128, 128), 128)], loc_sem.at[0])
    w_local.start()
    quarter = pl.ds(pl.multiple_of(x * 32, 32), 32)
    wo_local = pltpu.make_async_copy(w_out.at[quarter], wo.at[t, c, quarter], loc_sem.at[1])
    wo_local.start()

    v = tok[...].astype(F32)
    centred = v - jnp.mean(v, axis=-1, keepdims=True)
    spread = jnp.mean(centred * centred, axis=-1, keepdims=True)
    xg[t] = (centred * lax.rsqrt(spread + EPS) * ngain[...]).astype(BF)

    ri = lax.broadcasted_iota(jnp.int32, (256, 256), 0) // 64
    ci = lax.broadcasted_iota(jnp.int32, (256, 256), 1) // 64
    emat[...] = jnp.where(ri == ci, 1.0 / 64, 0.0).astype(BF)

    pl.semaphore_wait(barrier, len(partners))

    def ag_copy(src, dt, sem):
        return rcopy(xg.at[src], xg.at[src], ag_send.at[sem], ag_recv.at[src], (g, (t + dt) * 2 + c))

    @pl.when(t < 3)
    def _():
        ag_copy(t, 1, 0).start()

    @pl.when(t > 0)
    def _():
        ag_copy(t, -1, 1).start()

    w_cols = w3.at[:, :, pl.ds(pl.multiple_of(c * 128, 128), 128)]
    w_sib_cols = w3.at[:, :, pl.ds(pl.multiple_of((1 - c) * 128, 128), 128)]
    w_sib = rcopy(w, w_cols, ws_sem.at[0], ws_sem.at[1], sib)
    w_sib.start()

    half = t // 2
    near = t * (1 - half) + (3 - t) * half
    order = [t] + [a + half * (3 - 2 * a) for a in (1 - near, 2, 3)]

    def group_mean(a):
        hi = a.astype(BF)
        lo = (a - hi.astype(F32)).astype(BF)
        return dot(hi, emat[...]) + dot(lo, emat[...])

    def head_norm(a, gain):
        b = a - group_mean(a)
        return b * lax.rsqrt(group_mean(b * b) + EPS) * gain

    qg = jnp.concatenate([qgain[...]] * 4, axis=1)
    kg = jnp.concatenate([kgain[...]] * 4, axis=1)
    low = lax.broadcasted_iota(jnp.int32, (128, 128), 1) < 64

    def yq_copy(e, k):
        src = order[e]
        return rcopy(stq.at[e, (y + k) % 4], q_s.at[y, src], yq_send.at[e, k], yq_recv.at[e, k], y_dev(k))

    def yk_copy(e, k):
        src = order[e]
        return rcopy(stkv.at[e, (y + k) % 4], kv_s.at[y, src, c], yk_send.at[e, k], yk_recv.at[e, k], y_dev(k))

    def yq_wait(e, k):
        rcopy(stq.at[e, 0], q_s.at[(y + 4 - k) % 4, order[e]], yq_send.at[e, k], yq_recv.at[e, k], y_dev(k)).wait_recv()

    def yk_wait(e, k):
        rcopy(stkv.at[e, 0], kv_s.at[(y + 4 - k) % 4, order[e], c], yk_send.at[e, k], yk_recv.at[e, k], y_dev(k)).wait_recv()

    def project(e):
        src = order[e]
        h = xg[src]
        qn = head_norm(dot(h, w3[0]), qg)
        kn = head_norm(dot(h, w3[1]), kg)
        vn = dot(h, w3[2])
        for a in range(2):
            cols = slice(128 * a, 128 * a + 128)
            q2, k2, v2 = qn[:, cols], kn[:, cols], vn[:, cols]
            stq[e, 2 * a] = jnp.where(low, q2, 0.0).astype(BF)
            stq[e, 2 * a + 1] = jnp.where(low, pltpu.roll(q2, 64, 1), 0.0).astype(BF)
            stkv[e, 2 * a] = jnp.where(low, k2, pltpu.roll(v2, 64, 1)).astype(BF)
            stkv[e, 2 * a + 1] = jnp.where(low, pltpu.roll(k2, 64, 1), v2).astype(BF)
        for k in (1, 2, 3):
            yk_copy(e, k).start()
        for k in (1, 2, 3):
            yq_copy(e, k).start()
        q_s[y, src] = stq[e, y]
        kv_s[y, src, c] = stkv[e, y]

    def cross_copy(e, d):
        src = order[e]
        if d == 0:
            return rcopy(kv_s.at[pl.ds(1, 3), src, c], kvx.at[0, :, src, c], cr_send.at[e, 0], cr_recv.at[e, 0], up)
        return rcopy(kv_s.at[pl.ds(0, 3), src, c], kvx.at[1, :, src, c], cr_send.at[e, 1], cr_recv.at[e, 1], down)

    def sib_copy(e):
        src = order[e]
        return rcopy(kv_s.at[:, src, c], kv_s.at[:, src, c], sib_send.at[e], sib_recv.at[e], sib)

    def sib_wait(e):
        src = order[e]
        rcopy(kv_s.at[:, src, c], kv_s.at[:, src, 1 - c], sib_send.at[e], sib_recv.at[e], sib).wait_recv()

    def cs_copy(e, d):
        src = order[e]
        return rcopy(kvx.at[d, :, src, c], kvx.at[d, :, src, c], cs_send.at[e, d], cs_recv.at[e, d], sib)

    def cs_wait(e, d):
        src = order[e]
        rcopy(kvx.at[d, :, src, c], kvx.at[d, :, src, 1 - c], cs_send.at[e, d], cs_recv.at[e, d], sib).wait_recv()

    def spread_keys(e):
        for k in (1, 2, 3):
            yk_wait(e, k)
        for d in (0, 1):
            cross_copy(e, d).start()
        sib_copy(e).start()

    def cross_forward(e):
        for d in (0, 1):
            cross_copy(e, d).wait_recv()
            cs_copy(e, d).start()

    w_local.wait()
    rcopy(w, w_sib_cols, ws_sem.at[0], ws_sem.at[1], sib).wait_recv()
    project(0)
    for e in (1, 2, 3):
        src = order[e]
        rcopy(xg.at[src], xg.at[src], ag_send.at[0], ag_recv.at[src], sib).wait_recv()
        is_low = src < t

        @pl.when(is_low & (t < 3))
        def _():
            ag_copy(src, 1, e + 1).start()

        @pl.when(jnp.logical_not(is_low) & (t > 0))
        def _():
            ag_copy(src, -1, e + 1).start()

        spread_keys(e - 1)
        project(e)
    spread_keys(3)

    wo_local.wait()

    def wa_copy(m):
        return rcopy(
            wo.at[t, c, quarter], wo.at[t, c, quarter], wa_send.at[m], wa_recv.at[m], (g, ((t + m) % 4) * 2 + c)
        )

    def wb_copy(m):
        return rcopy(wo.at[:, c, quarter], wo.at[:, c, quarter], wb_send.at[m], wb_recv.at[m], x_dev(m))

    for m in (1, 2, 3):
        wa_copy(m).start()

    lane = lax.broadcasted_iota(jnp.int32, (1, 128), 1)
    ones_low = jnp.where(lane < 64, 1.0, 0.0).astype(BF)
    ones_high = jnp.where(lane < 64, 0.0, 1.0).astype(BF)

    def allowed(i, j, inside):
        jj = (j + 64) % 64
        ok = (covis[i, jj] == 1) & (rank[jj] <= rank[i]) & inside
        return jnp.where(ok, 1.0, 0.0).astype(F32)

    def block(yq, keys, mask):
        q = q_s[yq].reshape(512, 128)
        sc = lax.dot_general(q, keys, (((1,), (1,)), ((), ())), preferred_element_type=F32)
        p = jnp.exp2(sc * EXP_SCALE).astype(BF)
        va = keys * ones_high + ones_low
        return dot(p, va) * mask

    acc[...] = jnp.zeros_like(acc)
    for e in range(4):
        for k in (1, 2, 3):
            yq_wait(e, k)
    for e in range(4):
        sib_wait(e)

    def inner(i, _):
        yq = i % 4
        yk = i // 4
        keys = kv_s[yk].reshape(1024, 128)
        acc[yq] += block(yq, keys, allowed(base + yq, base + yk, True))
        return 0

    def cross(e):
        src = order[e]
        for d in (0, 1):
            cs_wait(e, d)
        for d in (0, 1):

            def step(p, _):
                m = 2 - p // 3 - p // 5
                yq = p - 3 * (p // 3) - 2 * (p // 5)
                if d == 0:
                    keys = kvx[0, m, src].reshape(256, 128)
                    mask = allowed(base + yq, base - 4 + m + 1, row > 0)
                else:
                    m, yq = 2 - m, 3 - yq
                    keys = kvx[1, m, src].reshape(256, 128)
                    mask = allowed(base + yq, base + 4 + m, row < 15)
                acc[yq] += block(yq, keys, mask)
                return 0

            lax.fori_loop(0, 6, step, 0)

    lax.fori_loop(0, 8, inner, 0)
    for m in (1, 2, 3):
        rcopy(
            wo.at[t, c, quarter], wo.at[(t + 4 - m) % 4, c, quarter], wa_send.at[m], wa_recv.at[m], sib
        ).wait_recv()
    for m in (1, 2, 3):
        wb_copy(m).start()
    cross_forward(0)
    lax.fori_loop(8, 16, inner, 0)
    cross_forward(1)
    cross(0)
    for m in (1, 2, 3):
        other = pl.ds(pl.multiple_of((x + 4 - m) % 4 * 32, 32), 32)
        rcopy(wo.at[:, c, quarter], wo.at[:, c, other], wb_send.at[m], wb_recv.at[m], sib).wait_recv()
    wc = rcopy(wo.at[:, c], wo.at[:, c], wc_sem.at[0], wc_sem.at[1], sib)
    wc.start()
    cross_forward(2)
    cross(1)
    cross(2)
    cross_forward(3)
    cross(3)

    low64 = lax.broadcasted_iota(jnp.int32, (64, 128), 1) < 64
    head = t * 4 + y
    for yq in range(4):
        for m in range(4):
            a = acc[yq, m * 128:(m + 1) * 128, :]
            r = pltpu.roll(a, 64, 1)
            top = r[:64] / a[:64]
            bottom = a[64:] / r[64:]
            fsend[yq, m] = jnp.where(low64, top, bottom).astype(BF)

    def f_copy(k, m):
        return rcopy(
            fsend.at[(y + k) % 4, (t + m) % 4], fin.at[head], f_send.at[k, m], f_recv.at[k, m], blk_dev(k, m)
        )

    def f_wait(k, m):
        other = ((t + 4 - m) % 4) * 4 + (y + 4 - k) % 4
        rcopy(fsend.at[0, 0], fin.at[other], f_send.at[k, m], f_recv.at[k, m], sib).wait_recv()

    order_f = [(k, m) for k in range(4) for m in range(4) if k or m]
    for k, m in order_f:
        f_copy(k, m).start()
    fin[head] = fsend[y, t]
    rcopy(wo.at[:, c], wo.at[:, 1 - c], wc_sem.at[0], wc_sem.at[1], sib).wait_recv()
    for k, m in order_f:
        f_wait(k, m)

    tops, bottoms = [], []
    for h in range(0, 16, 2):
        f0 = fin[h].astype(F32)
        f1 = fin[h + 1].astype(F32)
        tops.append(jnp.where(low64, f0, pltpu.roll(f1, 64, 1)).astype(BF))
        bottoms.append(jnp.where(low64, pltpu.roll(f0, 64, 1), f1).astype(BF))
    att = jnp.concatenate([jnp.concatenate(tops, axis=1), jnp.concatenate(bottoms, axis=1)], axis=0)
    out[...] = dot(att, wo[...].reshape(1024, 1024)).astype(BF)

    @pl.when(t < 3)
    def _():
        ag_copy(t, 1, 0).wait_send()

    @pl.when(t > 0)
    def _():
        ag_copy(t, -1, 1).wait_send()

    for e in (1, 2, 3):
        src = order[e]
        is_low = src < t

        @pl.when((is_low & (t < 3)) | (jnp.logical_not(is_low) & (t > 0)))
        def _():
            rcopy(xg.at[src], xg.at[src], ag_send.at[e + 1], ag_recv.at[src], sib).wait_send()

    w_sib.wait_send()
    for e in range(4):
        for k in (1, 2, 3):
            yq_copy(e, k).wait_send()
            yk_copy(e, k).wait_send()
        for d in (0, 1):
            cross_copy(e, d).wait_send()
            cs_copy(e, d).wait_send()
        sib_copy(e).wait_send()
    for m in (1, 2, 3):
        wa_copy(m).wait_send()
        wb_copy(m).wait_send()
    wc.wait_send()
    for k, m in order_f:
        f_copy(k, m).wait_send()


def body(tokens, norm_gain, w_qkv, q_gain, k_gain, w_out, covis_mask, capture_rank):
    vm = pl.BlockSpec(memory_space=pltpu.VMEM)
    sm = pl.BlockSpec(memory_space=pltpu.SMEM)
    hbm = pl.BlockSpec(memory_space=pl.ANY)
    dma = pltpu.SemaphoreType.DMA
    result = pl.pallas_call(
        kernel,
        out_shape=jax.ShapeDtypeStruct((128, 1024), BF),
        in_specs=[vm, vm, hbm, vm, vm, hbm, sm, sm],
        out_specs=vm,
        scratch_shapes=[
            pltpu.VMEM((4, 128, 1024), BF),
            pltpu.VMEM((3, 1024, 256), BF),
            pltpu.VMEM((256, 256), BF),
            pltpu.VMEM((4, 4, 128, 128), BF),
            pltpu.VMEM((4, 4, 128, 128), BF),
            pltpu.VMEM((4, 4, 128, 128), BF),
            pltpu.VMEM((4, 4, 2, 128, 128), BF),
            pltpu.VMEM((2, 3, 4, 2, 128, 128), BF),
            pltpu.VMEM((4, 512, 128), F32),
            pltpu.VMEM((4, 2, 128, 1024), BF),
            pltpu.VMEM((16, 64, 128), BF),
            pltpu.VMEM((4, 4, 64, 128), BF),
            dma((2,)), dma((2,)), dma((5,)), dma((4,)),
            dma((4, 4)), dma((4, 4)), dma((4, 4)), dma((4, 4)),
            dma((4,)), dma((4,)), dma((4, 2)), dma((4, 2)), dma((4, 2)), dma((4, 2)),
            dma((4,)), dma((4,)), dma((4,)), dma((4,)), dma((2,)), dma((4, 4)), dma((4, 4)),
        ],
        compiler_params=pltpu.CompilerParams(
            collective_id=0, has_side_effects=True, vmem_limit_bytes=40 * 1024 * 1024
        ),
        cost_estimate=pl.CostEstimate(flops=10_000_000_000, bytes_accessed=4_000_000, transcendentals=15_000_000),
    )(
        tokens[0],
        norm_gain.reshape(1, 1024),
        jnp.transpose(w_qkv, (1, 0, 2)),
        q_gain.reshape(1, 64),
        k_gain.reshape(1, 64),
        w_out,
        covis_mask,
        capture_rank,
    )
    return result[None]


def solution(mesh):
    placed = (
        P("group", "slab", None),
        P(),
        P(None, None, "slab"),
        P(),
        P(),
        P("slab", None),
        P(),
        P(),
    )
    return jax.shard_map(
        body, mesh=mesh, in_specs=placed, out_specs=P("group", "slab", None), check_vma=False
    )
```

```python
import functools
import math

import jax
import jax.numpy as jnp
from jax import lax
from jax.experimental import pallas as pl
from jax.experimental.pallas import tpu as pltpu
from jax.sharding import PartitionSpec as P

MESH = pl.DeviceIdType.MESH
BF = jnp.bfloat16
F32 = jnp.float32
EPS = 1e-06
EXP_SCALE = 0.125 * math.log2(math.e)


def dot(a, b):
    return jnp.dot(a, b, preferred_element_type=F32)


def kernel(
    tok_h, ngain_h, w, qgain_h, kgain_h, w_out, covis_h, rank_h, out,
    tok, ngain, qgain, kgain, covis, rank, xg, w3, emat, stq, stkv, q_s, kvr, kvx, acc, wo, fin, fsend,
    loc_sem, ws_sem, ag_send, ag_recv, yq_send, yq_recv, yk_send, yk_recv, sib_send, sib_recv,
    wa_send, wa_recv, wy_send, wy_recv, wb_send, wb_recv, wc_sem, f_send, f_recv,
):
    g = lax.axis_index("group")
    s = lax.axis_index("slab")
    y = g % 4
    base = (g // 4) * 4
    x = g // 16
    zy = g % 16
    t = s // 2
    c = s % 2
    sib = (g, t * 2 + 1 - c)

    def y_dev(k):
        return (base + (y + k) % 4, s)

    def blk_dev(k, m):
        return (base + (y + k) % 4, ((t + m) % 4) * 2 + c)

    def x_dev(k):
        return (((x + k) % 4) * 16 + zy, s)

    def rcopy(src, dst, ss, rs, dev):
        return pltpu.make_async_remote_copy(
            src_ref=src, dst_ref=dst, send_sem=ss, recv_sem=rs, device_id=dev, device_id_type=MESH
        )

    def reach(d):
        return t * (1 - d) + (3 - t) * d

    def column(a, d):
        return a * (1 - d) + (3 - a) * d

    def slot(k, d):
        return 4 + t + (2 * d - 1) * k

    def next_dev(d):
        sign = 2 * d - 1
        edge = reach(d) // 3
        return ((g + 64 - 4 * sign * edge) % 64, s - 2 * sign + 8 * sign * edge)

    loads = [
        pltpu.make_async_copy(src, dst, loc_sem.at[2 + i])
        for i, (src, dst) in enumerate(
            [(tok_h, tok), (ngain_h, ngain), (qgain_h, qgain), (kgain_h, kgain), (covis_h, covis), (rank_h, rank)]
        )
    ]
    for copy in loads:
        copy.start()

    barrier = pltpu.get_barrier_semaphore()
    partners = [next_dev(0), next_dev(1), sib] + [y_dev(k) for k in (1, 2, 3)] + [x_dev(k) for k in (1, 2, 3)]
    for dev in partners:
        pl.semaphore_signal(barrier, inc=1, device_id=dev, device_id_type=MESH)

    own_cols = pl.ds(pl.multiple_of(c * 128, 128), 128)
    w_local = pltpu.make_async_copy(w, w3.at[:, :, own_cols], loc_sem.at[0])
    w_local.start()
    quarter = pl.ds(pl.multiple_of(x * 32, 32), 32)

    def part(a):
        return pl.ds(pl.multiple_of(a * 256, 256), 256)

    wo_local = pltpu.make_async_copy(
        w_out.at[quarter, part(y)], wo.at[t, c, quarter, part(y)], loc_sem.at[1]
    )
    wo_local.start()

    loads[0].wait()
    loads[1].wait()
    v = tok[...].astype(F32)
    centred = v - jnp.mean(v, axis=-1, keepdims=True)
    spread = jnp.mean(centred * centred, axis=-1, keepdims=True)
    xg[4 + t] = (centred * lax.rsqrt(spread + EPS) * ngain[...]).astype(BF)

    ri = lax.broadcasted_iota(jnp.int32, (256, 256), 0) // 64
    ci = lax.broadcasted_iota(jnp.int32, (256, 256), 1) // 64
    emat[...] = jnp.where(ri == ci, 1.0 / 64, 0.0).astype(BF)

    pl.semaphore_wait(barrier, len(partners))

    def pass_on(k, d, sem):
        here = slot(k, d)
        there = here + 4 * (2 * d - 1) * (reach(d) // 3)
        return rcopy(xg.at[here], xg.at[there], ag_send.at[sem], ag_recv.at[there], next_dev(d))

    def passes_on(k, d):
        return (reach(d) < 3) | ((k <= reach(d)) & (column(y, d) >= 1))

    def arrives(k, d):
        return (k <= reach(d)) | ((k <= reach(d) + 4) & (column(y, d) >= 1))

    for d in (0, 1):

        @pl.when(passes_on(0, d))
        def _():
            pass_on(0, d, 12 + d).start()

    def wa_copy(m):
        piece = wo.at[t, c, quarter, part(y)]
        return rcopy(piece, piece, wa_send.at[m], wa_recv.at[m], (g, ((t + m) % 4) * 2 + c))

    def wy_copy(m):
        piece = wo.at[:, c, quarter, part(y)]
        return rcopy(piece, piece, wy_send.at[m], wy_recv.at[m], y_dev(m))

    def wb_copy(m):
        piece = wo.at[:, c, quarter]
        return rcopy(piece, piece, wb_send.at[m], wb_recv.at[m], x_dev(m))

    wc = rcopy(wo.at[:, c], wo.at[:, c], wc_sem.at[0], wc_sem.at[1], sib)

    def wa_wait(m):
        piece = wo.at[t, c, quarter, part(y)]
        rcopy(piece, wo.at[(t + 4 - m) % 4, c, quarter, part(y)], wa_send.at[m], wa_recv.at[m], sib).wait_recv()

    def wy_wait(m):
        piece = wo.at[:, c, quarter, part(y)]
        rcopy(piece, wo.at[:, c, quarter, part((y + 4 - m) % 4)], wy_send.at[m], wy_recv.at[m], sib).wait_recv()

    def wb_wait(m):
        other = pl.ds(pl.multiple_of((x + 4 - m) % 4 * 32, 32), 32)
        rcopy(wo.at[:, c, quarter], wo.at[:, c, other], wb_send.at[m], wb_recv.at[m], sib).wait_recv()

    def w_out_stage(wait, start):
        for m in (1, 2, 3):
            wait(m)
        for m in (1, 2, 3):
            start(m).start()

    w_sib = rcopy(w, w3.at[:, :, own_cols], ws_sem.at[0], ws_sem.at[1], sib)
    w_sib.start()
    for copy in loads[2:]:
        copy.wait()

    def group_mean(a):
        hi = a.astype(BF)
        lo = (a - hi.astype(F32)).astype(BF)
        return dot(hi, emat[...]) + dot(lo, emat[...])

    def head_norm(a, gain):
        b = a - group_mean(a)
        return b * lax.rsqrt(group_mean(b * b) + EPS) * gain

    qg = jnp.concatenate([qgain[...]] * 4, axis=1)
    kg = jnp.concatenate([kgain[...]] * 4, axis=1)
    low = lax.broadcasted_iota(jnp.int32, (128, 128), 1) < 64

    def yq_copy(z, k):
        return rcopy(stq.at[z - 4, (y + k) % 4], q_s.at[y, z - 4], yq_send.at[z - 4, k], yq_recv.at[z - 4, k], y_dev(k))

    def row_copy(z, k):
        return rcopy(
            stkv.at[z, (y + k) % 4], kvr.at[y, z - 4, c], yk_send.at[z, k], yk_recv.at[z, k], y_dev(k)
        )

    def cross_copy(z, d, k):
        return rcopy(
            stkv.at[z, (y + k) % 4], kvx.at[d, column(y, d) - 1, z % 4, c], yk_send.at[z, k], yk_recv.at[z, k], y_dev(k)
        )

    def yq_wait(z, k):
        rcopy(
            stq.at[0, 0], q_s.at[(y + 4 - k) % 4, z - 4], yq_send.at[z - 4, k], yq_recv.at[z - 4, k], sib
        ).wait_recv()

    def row_wait(z, k):
        rcopy(stkv.at[0, 0], kvr.at[(y + 4 - k) % 4, z - 4, c], yk_send.at[z, k], yk_recv.at[z, k], sib).wait_recv()

    def cross_wait(z, d, k):
        m = column((y + 4 - k) % 4, d) - 1
        rcopy(stkv.at[0, 0], kvx.at[d, m, z % 4, c], yk_send.at[z, k], yk_recv.at[z, k], sib).wait_recv()

    def project_keys(z):
        h = xg[z]
        kn = head_norm(dot(h, w3[1]), kg)
        vn = dot(h, w3[2])
        for a in range(2):
            cols = slice(128 * a, 128 * a + 128)
            k2, v2 = kn[:, cols], vn[:, cols]
            stkv[z, 2 * a] = jnp.where(low, k2, pltpu.roll(v2, 64, 1)).astype(BF)
            stkv[z, 2 * a + 1] = jnp.where(low, pltpu.roll(k2, 64, 1), v2).astype(BF)

    def project_queries(z):
        qn = head_norm(dot(xg[z], w3[0]), qg)
        for a in range(2):
            q2 = qn[:, 128 * a:128 * a + 128]
            stq[z - 4, 2 * a] = jnp.where(low, q2, 0.0).astype(BF)
            stq[z - 4, 2 * a + 1] = jnp.where(low, pltpu.roll(q2, 64, 1), 0.0).astype(BF)
        for k in (1, 2, 3):
            yq_copy(z, k).start()
        q_s[y, z - 4] = stq[z - 4, y]

    def project_row(z):
        project_keys(z)
        for k in (1, 2, 3):
            row_copy(z, k).start()
        kvr[y, z - 4, c] = stkv[z, y]
        project_queries(z)

    def project_cross(z, d):
        project_keys(z)
        for k in (1, 2, 3):
            cross_copy(z, d, k).start()
        kvx[d, column(y, d) - 1, z % 4, c] = stkv[z, y]

    def row_sib(z):
        return rcopy(kvr.at[:, z - 4, c], kvr.at[:, z - 4, c], sib_send.at[z], sib_recv.at[z], sib)

    def row_sib_wait(z):
        rcopy(kvr.at[:, z - 4, c], kvr.at[:, z - 4, 1 - c], sib_send.at[z], sib_recv.at[z], sib).wait_recv()

    def cross_sib(z, d):
        return rcopy(kvx.at[d, :, z % 4, c], kvx.at[d, :, z % 4, c], sib_send.at[z], sib_recv.at[z], sib)

    def cross_sib_wait(z, d):
        rcopy(kvx.at[d, :, z % 4, c], kvx.at[d, :, z % 4, 1 - c], sib_send.at[z], sib_recv.at[z], sib).wait_recv()

    def row_arrived(z):
        for k in (1, 2, 3):
            row_wait(z, k)
        row_sib(z).start()
        for k in (1, 2, 3):
            yq_wait(z, k)

    def is_row(k, d):
        return k <= reach(d)

    def is_cross(k, d):
        return (k > reach(d)) & (k <= reach(d) + 4)

    def spread_keys(k, d):
        z = slot(k, d)

        @pl.when(is_row(k, d))
        def _():
            row_arrived(z)

        @pl.when(is_cross(k, d))
        def _():
            for n in (1, 2, 3):

                @pl.when(column((y + 4 - n) % 4, d) >= 1)
                def _():
                    cross_wait(z, d, n)

            cross_sib(z, d).start()

    lane = lax.broadcasted_iota(jnp.int32, (1, 128), 1)
    ones_low = jnp.where(lane < 64, 1.0, 0.0).astype(BF)
    ones_high = jnp.where(lane < 64, 0.0, 1.0).astype(BF)

    def allowed(i, j):
        jj = (j + 64) % 64
        ok = (covis[i, jj] == 1) & (rank[jj] <= rank[i]) & (j >= 0) & (j < 64)
        return jnp.where(ok, 1.0, 0.0).astype(F32)

    def block(q, keys):
        sc = lax.dot_general(q, keys, (((1,), (1,)), ((), ())), preferred_element_type=F32)
        p = jnp.exp2(sc * EXP_SCALE).astype(BF)
        va = keys * ones_high + ones_low
        return dot(p, va)

    def own_image(i, _):
        acc[i] = block(q_s[i].reshape(512, 128), kvr[i].reshape(1024, 128)) * allowed(base + i, base + i)
        return 0

    def pair(p):
        m = 2 - p // 3 - p // 5
        return p - 3 * (p // 3) - 2 * (p // 5), m

    def row_pair(p, _):
        a, m = pair(p)
        b = m + 1
        ab = allowed(base + a, base + b)
        ba = allowed(base + b, base + a)
        q_of = jnp.where(ab > 0.5, a, b)
        r = block(q_s[q_of].reshape(512, 128), kvr[a + b - q_of].reshape(1024, 128))
        acc[a] += r * ab
        acc[b] += r * ba
        return 0

    def cross(d, yq, m, first, count):
        i = column(yq, d)
        j = (m - 3) * (1 - d) + (6 - m) * d
        keys = kvx[d, m, pl.ds(first, count)].reshape(256 * count, 128)
        acc[i] += block(q_s[i].reshape(512, 128), keys) * allowed(base + i, base + j)

    near = t // 2
    far = 1 - near

    def near_pair(p, _):
        a, m = pair(p)
        cross(near, a, m, 0, 4)
        return 0

    def far_pair(p, _):
        a, m = pair(p)
        cross(far, a, m, 1 - far, 3)
        return 0

    w_local.wait()
    other_cols = pl.ds(pl.multiple_of((1 - c) * 128, 128), 128)
    rcopy(w, w3.at[:, :, other_cols], ws_sem.at[0], ws_sem.at[1], sib).wait_recv()
    project_row(4 + t)

    def z_step(k, _):
        def forward(d, _):
            z = slot(k, d)

            @pl.when(arrives(k, d))
            def _():
                rcopy(xg.at[z], xg.at[z], ag_send.at[z], ag_recv.at[z], sib).wait_recv()

                @pl.when(passes_on(k, d))
                def _():
                    pass_on(k, d, z).start()

            return 0

        lax.fori_loop(0, 2, forward, 0)

        @pl.when(k == 1)
        def _():
            row_arrived(4 + t)

        @pl.when(k == 3)
        def _():
            wo_local.wait()
            for m in (1, 2, 3):
                wa_copy(m).start()

        @pl.when(k == 4)
        def _():
            w_out_stage(wa_wait, wy_copy)

        @pl.when(k == 5)
        def _():
            w_out_stage(wy_wait, wb_copy)

        def project(d, _):
            z = slot(k, d)

            @pl.when(arrives(k, d))
            def _():
                @pl.when(is_row(k, d))
                def _():
                    project_row(z)

                @pl.when(is_cross(k, d))
                def _():
                    project_cross(z, d)

            return 0

        lax.fori_loop(0, 2, project, 0)

        @pl.when(k == 4)
        def _():
            for e in range(4):
                row_sib_wait(4 + e)
            lax.fori_loop(0, 4, own_image, 0)

        @pl.when(k == 5)
        def _():
            lax.fori_loop(0, 4, row_pair, 0)

        @pl.when(k == 6)
        def _():
            lax.fori_loop(4, 6, row_pair, 0)
            for e in range(4):
                cross_sib_wait(8 * near + e, near)
            lax.fori_loop(0, 2, near_pair, 0)

        @pl.when(k == 7)
        def _():
            lax.fori_loop(2, 6, near_pair, 0)

        def spread_step(d, _):
            spread_keys(k, d)
            return 0

        lax.fori_loop(0, 2, spread_step, 0)
        return 0

    lax.fori_loop(1, 8, z_step, 0)
    for m in (1, 2, 3):
        wb_wait(m)
    wc.start()
    for e in range(3):
        cross_sib_wait(8 * far + 1 - far + e, far)
    lax.fori_loop(0, 6, far_pair, 0)

    low64 = lax.broadcasted_iota(jnp.int32, (64, 128), 1) < 64
    head = t * 4 + y

    def f_copy(k, m):
        return rcopy(
            fsend.at[(y + k) % 4, (t + m) % 4], fin.at[head], f_send.at[k, m], f_recv.at[k, m], blk_dev(k, m)
        )

    def f_wait(k, m):
        other = ((t + 4 - m) % 4) * 4 + (y + 4 - k) % 4
        rcopy(fsend.at[0, 0], fin.at[other], f_send.at[k, m], f_recv.at[k, m], sib).wait_recv()

    def finish(a):
        i = column(a, far)
        for m in range(4):
            n = acc[i, m * 128:(m + 1) * 128, :]
            r = pltpu.roll(n, 64, 1)
            top = r[:64] / n[:64]
            bottom = n[64:] / r[64:]
            fsend[i, m] = jnp.where(low64, top, bottom).astype(BF)
        k = (i + 4 - y) % 4
        for m in range(1, 4):
            f_copy(k, m).start()

        @pl.when(k > 0)
        def _():
            f_copy(k, 0).start()

    finish(3)
    cross_sib_wait(11 * far, far)
    for a in (2, 1, 0):
        for m in range(a, 3):
            cross(far, a, m, 3 * far, 1)
        finish(a)
    fin[head] = fsend[y, t]
    order_f = [(k, m) for k in range(4) for m in range(4) if k or m]
    rcopy(wo.at[:, c], wo.at[:, 1 - c], wc_sem.at[0], wc_sem.at[1], sib).wait_recv()
    for k, m in order_f:
        f_wait(k, m)

    tops, bottoms = [], []
    for h in range(0, 16, 2):
        f0 = fin[h].astype(F32)
        f1 = fin[h + 1].astype(F32)
        tops.append(jnp.where(low64, f0, pltpu.roll(f1, 64, 1)).astype(BF))
        bottoms.append(jnp.where(low64, pltpu.roll(f0, 64, 1), f1).astype(BF))
    att = jnp.concatenate([jnp.concatenate(tops, axis=1), jnp.concatenate(bottoms, axis=1)], axis=0)
    out[...] = dot(att, wo[...].reshape(1024, 1024)).astype(BF)

    for d in (0, 1):

        @pl.when(passes_on(0, d))
        def _():
            pass_on(0, d, 12 + d).wait_send()

    w_sib.wait_send()
    for m in (1, 2, 3):
        wa_copy(m).wait_send()
        wy_copy(m).wait_send()
        wb_copy(m).wait_send()
    wc.wait_send()

    def row_sent(z):
        for n in (1, 2, 3):
            row_copy(z, n).wait_send()
            yq_copy(z, n).wait_send()
        row_sib(z).wait_send()

    row_sent(4 + t)

    def sent(i, _):
        k = 1 + i // 2
        d = i % 2
        z = slot(k, d)

        @pl.when(arrives(k, d) & passes_on(k, d))
        def _():
            pass_on(k, d, z).wait_send()

        @pl.when(is_row(k, d))
        def _():
            row_sent(z)

        @pl.when(is_cross(k, d))
        def _():
            @pl.when(column(y, d) >= 1)
            def _():
                for n in (1, 2, 3):
                    cross_copy(z, d, n).wait_send()

            cross_sib(z, d).wait_send()

        return 0

    lax.fori_loop(0, 14, sent, 0)
    for k, m in order_f:
        f_copy(k, m).wait_send()


def body(tokens, norm_gain, w_qkv, q_gain, k_gain, w_out, covis_mask, capture_rank):
    vm = pl.BlockSpec(memory_space=pltpu.VMEM)
    hbm = pl.BlockSpec(memory_space=pl.ANY)
    dma = pltpu.SemaphoreType.DMA
    result = pl.pallas_call(
        kernel,
        out_shape=jax.ShapeDtypeStruct((128, 1024), BF),
        in_specs=[hbm] * 8,
        out_specs=vm,
        scratch_shapes=[
            pltpu.VMEM((128, 1024), BF),
            pltpu.VMEM((1, 1024), F32),
            pltpu.VMEM((1, 64), F32),
            pltpu.VMEM((1, 64), F32),
            pltpu.SMEM((64, 64), jnp.int32),
            pltpu.SMEM((64,), jnp.int32),
            pltpu.VMEM((12, 128, 1024), BF),
            pltpu.VMEM((3, 1024, 256), BF),
            pltpu.VMEM((256, 256), BF),
            pltpu.VMEM((4, 4, 128, 128), BF),
            pltpu.VMEM((12, 4, 128, 128), BF),
            pltpu.VMEM((4, 4, 128, 128), BF),
            pltpu.VMEM((4, 4, 2, 128, 128), BF),
            pltpu.VMEM((2, 3, 4, 2, 128, 128), BF),
            pltpu.VMEM((4, 512, 128), F32),
            pltpu.VMEM((4, 2, 128, 1024), BF),
            pltpu.VMEM((16, 64, 128), BF),
            pltpu.VMEM((4, 4, 64, 128), BF),
            dma((8,)), dma((2,)), dma((14,)), dma((12,)),
            dma((4, 4)), dma((4, 4)), dma((12, 4)), dma((12, 4)), dma((12,)), dma((12,)),
            dma((4,)), dma((4,)), dma((4,)), dma((4,)), dma((4,)), dma((4,)), dma((2,)), dma((4, 4)), dma((4, 4)),
        ],
        compiler_params=pltpu.CompilerParams(
            collective_id=0, has_side_effects=True, vmem_limit_bytes=60 * 1024 * 1024
        ),
        cost_estimate=pl.CostEstimate(flops=10_000_000_000, bytes_accessed=4_000_000, transcendentals=15_000_000),
    )(
        tokens[0],
        norm_gain.reshape(1, 1024),
        jnp.transpose(w_qkv, (1, 0, 2)),
        q_gain.reshape(1, 64),
        k_gain.reshape(1, 64),
        w_out,
        covis_mask,
        capture_rank,
    )
    return result[None]


def solution(mesh):
    placed = (
        P("group", "slab", None),
        P(),
        P(None, None, "slab"),
        P(),
        P(),
        P("slab", None),
        P(),
        P(),
    )
    return jax.shard_map(
        body, mesh=mesh, in_specs=placed, out_specs=P("group", "slab", None), check_vma=False
    )
```

```python
import functools
import math

import jax
import jax.numpy as jnp
from jax import lax
from jax.experimental import pallas as pl
from jax.experimental.pallas import tpu as pltpu
from jax.sharding import PartitionSpec as P

MESH = pl.DeviceIdType.MESH
BF = jnp.bfloat16
F32 = jnp.float32
EPS = 1e-06
EXP_SCALE = 0.125 * math.log2(math.e)


def dot(a, b):
    return jnp.dot(a, b, preferred_element_type=F32)


def kernel(
    tok_h, ngain_h, w, qgain_h, kgain_h, w_out, covis_h, rank_h, out,
    tok, ngain, qgain, kgain, covis, rank, xg, w3, emat, stq, stkv, q_s, kvr, kvx, acc, wo, fin, fsend,
    loc_sem, ws_sem, ag_send, ag_recv, yq_send, yq_recv, yk_send, yk_recv, sib_send, sib_recv,
    wa_send, wa_recv, wy_send, wy_recv, wb_send, wb_recv, wc_sem, f_send, f_recv,
):
    g = lax.axis_index("group")
    s = lax.axis_index("slab")
    y = g % 4
    base = (g // 4) * 4
    x = g // 16
    zy = g % 16
    t = s // 2
    c = s % 2
    sib = (g, t * 2 + 1 - c)

    def y_dev(k):
        return (base + (y + k) % 4, s)

    def blk_dev(k, m):
        return (base + (y + k) % 4, ((t + m) % 4) * 2 + c)

    def x_dev(k):
        return (((x + k) % 4) * 16 + zy, s)

    def rcopy(src, dst, ss, rs, dev):
        return pltpu.make_async_remote_copy(
            src_ref=src, dst_ref=dst, send_sem=ss, recv_sem=rs, device_id=dev, device_id_type=MESH
        )

    def reach(d):
        return t * (1 - d) + (3 - t) * d

    def column(a, d):
        return a * (1 - d) + (3 - a) * d

    def slot(k, d):
        return 4 + t + (2 * d - 1) * k

    def next_dev(d):
        sign = 2 * d - 1
        edge = reach(d) // 3
        return ((g + 64 - 4 * sign * edge) % 64, s - 2 * sign + 8 * sign * edge)

    loads = [
        pltpu.make_async_copy(src, dst, loc_sem.at[2 + i])
        for i, (src, dst) in enumerate(
            [(tok_h, tok), (ngain_h, ngain), (qgain_h, qgain), (kgain_h, kgain), (covis_h, covis), (rank_h, rank)]
        )
    ]
    for copy in loads:
        copy.start()

    barrier = pltpu.get_barrier_semaphore()
    partners = [next_dev(0), next_dev(1), sib] + [y_dev(k) for k in (1, 2, 3)] + [x_dev(k) for k in (1, 2, 3)]
    for dev in partners:
        pl.semaphore_signal(barrier, inc=1, device_id=dev, device_id_type=MESH)

    own_cols = pl.ds(pl.multiple_of(c * 128, 128), 128)
    w_local = pltpu.make_async_copy(w, w3.at[:, :, own_cols], loc_sem.at[0])
    w_local.start()
    quarter = pl.ds(pl.multiple_of(x * 32, 32), 32)

    def part(a):
        return pl.ds(pl.multiple_of(a * 256, 256), 256)

    wo_local = pltpu.make_async_copy(
        w_out.at[quarter, part(y)], wo.at[t, c, quarter, part(y)], loc_sem.at[1]
    )
    wo_local.start()

    loads[0].wait()
    loads[1].wait()
    v = tok[...].astype(F32)
    centred = v - jnp.mean(v, axis=-1, keepdims=True)
    spread = jnp.mean(centred * centred, axis=-1, keepdims=True)
    xg[4 + t] = (centred * lax.rsqrt(spread + EPS) * ngain[...]).astype(BF)

    ri = lax.broadcasted_iota(jnp.int32, (256, 256), 0) // 64
    ci = lax.broadcasted_iota(jnp.int32, (256, 256), 1) // 64
    emat[...] = jnp.where(ri == ci, 1.0 / 64, 0.0).astype(BF)

    pl.semaphore_wait(barrier, len(partners))

    def half_of(z, h):
        return xg.at[z, pl.ds(pl.multiple_of(64 * h, 64), 64)]

    def pass_on(k, d, h, sem):
        here = slot(k, d)
        there = here + 4 * (2 * d - 1) * (reach(d) // 3)
        return rcopy(half_of(here, h), half_of(there, h), ag_send.at[sem, h], ag_recv.at[there, h], next_dev(d))

    def passes_on(k, d):
        return (reach(d) < 3) | ((k <= reach(d)) & (column(y, d) >= 1))

    def arrives(k, d):
        return (k <= reach(d)) | ((k <= reach(d) + 4) & (column(y, d) >= 1))

    for d in (0, 1):

        @pl.when(passes_on(0, d))
        def _():
            for h in (0, 1):
                pass_on(0, d, h, 12 + d).start()

    def wa_copy(m):
        piece = wo.at[t, c, quarter, part(y)]
        return rcopy(piece, piece, wa_send.at[m], wa_recv.at[m], (g, ((t + m) % 4) * 2 + c))

    def wy_copy(m):
        piece = wo.at[:, c, quarter, part(y)]
        return rcopy(piece, piece, wy_send.at[m], wy_recv.at[m], y_dev(m))

    def wb_copy(m):
        piece = wo.at[:, c, quarter]
        return rcopy(piece, piece, wb_send.at[m], wb_recv.at[m], x_dev(m))

    wc = rcopy(wo.at[:, c], wo.at[:, c], wc_sem.at[0], wc_sem.at[1], sib)

    def wa_wait(m):
        piece = wo.at[t, c, quarter, part(y)]
        rcopy(piece, wo.at[(t + 4 - m) % 4, c, quarter, part(y)], wa_send.at[m], wa_recv.at[m], sib).wait_recv()

    def wy_wait(m):
        piece = wo.at[:, c, quarter, part(y)]
        rcopy(piece, wo.at[:, c, quarter, part((y + 4 - m) % 4)], wy_send.at[m], wy_recv.at[m], sib).wait_recv()

    def wb_wait(m):
        other = pl.ds(pl.multiple_of((x + 4 - m) % 4 * 32, 32), 32)
        rcopy(wo.at[:, c, quarter], wo.at[:, c, other], wb_send.at[m], wb_recv.at[m], sib).wait_recv()

    def w_out_stage(wait, start):
        for m in (1, 2, 3):
            wait(m)
        for m in (1, 2, 3):
            start(m).start()

    w_sib = rcopy(w, w3.at[:, :, own_cols], ws_sem.at[0], ws_sem.at[1], sib)
    w_sib.start()
    for copy in loads[2:]:
        copy.wait()

    def group_mean(a):
        hi = a.astype(BF)
        lo = (a - hi.astype(F32)).astype(BF)
        return dot(hi, emat[...]) + dot(lo, emat[...])

    def head_norm(a, gain):
        b = a - group_mean(a)
        return b * lax.rsqrt(group_mean(b * b) + EPS) * gain

    qg = jnp.concatenate([qgain[...]] * 4, axis=1)
    kg = jnp.concatenate([kgain[...]] * 4, axis=1)
    low = lax.broadcasted_iota(jnp.int32, (128, 128), 1) < 64

    def yq_copy(z, k):
        return rcopy(stq.at[z - 4, (y + k) % 4], q_s.at[y, z - 4], yq_send.at[z - 4, k], yq_recv.at[z - 4, k], y_dev(k))

    def row_copy(z, k):
        return rcopy(
            stkv.at[z, (y + k) % 4], kvr.at[y, z - 4, c], yk_send.at[z, k], yk_recv.at[z, k], y_dev(k)
        )

    def cross_copy(z, d, k):
        return rcopy(
            stkv.at[z, (y + k) % 4], kvx.at[d, column(y, d) - 1, z % 4, c], yk_send.at[z, k], yk_recv.at[z, k], y_dev(k)
        )

    def yq_wait(z, k):
        rcopy(
            stq.at[0, 0], q_s.at[(y + 4 - k) % 4, z - 4], yq_send.at[z - 4, k], yq_recv.at[z - 4, k], sib
        ).wait_recv()

    def row_wait(z, k):
        rcopy(stkv.at[0, 0], kvr.at[(y + 4 - k) % 4, z - 4, c], yk_send.at[z, k], yk_recv.at[z, k], sib).wait_recv()

    def cross_wait(z, d, k):
        m = column((y + 4 - k) % 4, d) - 1
        rcopy(stkv.at[0, 0], kvx.at[d, m, z % 4, c], yk_send.at[z, k], yk_recv.at[z, k], sib).wait_recv()

    def project_keys(z):
        h = xg[z]
        kn = head_norm(dot(h, w3[1]), kg)
        vn = dot(h, w3[2])
        for a in range(2):
            cols = slice(128 * a, 128 * a + 128)
            k2, v2 = kn[:, cols], vn[:, cols]
            stkv[z, 2 * a] = jnp.where(low, k2, pltpu.roll(v2, 64, 1)).astype(BF)
            stkv[z, 2 * a + 1] = jnp.where(low, pltpu.roll(k2, 64, 1), v2).astype(BF)

    def project_queries(z):
        qn = head_norm(dot(xg[z], w3[0]), qg)
        for a in range(2):
            q2 = qn[:, 128 * a:128 * a + 128]
            stq[z - 4, 2 * a] = jnp.where(low, q2, 0.0).astype(BF)
            stq[z - 4, 2 * a + 1] = jnp.where(low, pltpu.roll(q2, 64, 1), 0.0).astype(BF)
        for k in (1, 2, 3):
            yq_copy(z, k).start()
        q_s[y, z - 4] = stq[z - 4, y]

    def project_row(z):
        project_keys(z)
        for k in (1, 2, 3):
            row_copy(z, k).start()
        kvr[y, z - 4, c] = stkv[z, y]
        project_queries(z)

    def project_cross(z, d):
        project_keys(z)
        for k in (1, 2, 3):
            cross_copy(z, d, k).start()
        kvx[d, column(y, d) - 1, z % 4, c] = stkv[z, y]

    def row_sib(z):
        return rcopy(kvr.at[:, z - 4, c], kvr.at[:, z - 4, c], sib_send.at[z], sib_recv.at[z], sib)

    def row_sib_wait(z):
        rcopy(kvr.at[:, z - 4, c], kvr.at[:, z - 4, 1 - c], sib_send.at[z], sib_recv.at[z], sib).wait_recv()

    def cross_sib(z, d):
        return rcopy(kvx.at[d, :, z % 4, c], kvx.at[d, :, z % 4, c], sib_send.at[z], sib_recv.at[z], sib)

    def cross_sib_wait(z, d):
        rcopy(kvx.at[d, :, z % 4, c], kvx.at[d, :, z % 4, 1 - c], sib_send.at[z], sib_recv.at[z], sib).wait_recv()

    def row_arrived(z):
        for k in (1, 2, 3):
            row_wait(z, k)
        row_sib(z).start()
        for k in (1, 2, 3):
            yq_wait(z, k)

    def is_row(k, d):
        return k <= reach(d)

    def is_cross(k, d):
        return (k > reach(d)) & (k <= reach(d) + 4)

    def spread_keys(k, d):
        z = slot(k, d)

        @pl.when(is_row(k, d))
        def _():
            row_arrived(z)

        @pl.when(is_cross(k, d))
        def _():
            for n in (1, 2, 3):

                @pl.when(column((y + 4 - n) % 4, d) >= 1)
                def _():
                    cross_wait(z, d, n)

            cross_sib(z, d).start()

    lane = lax.broadcasted_iota(jnp.int32, (1, 128), 1)
    ones_low = jnp.where(lane < 64, 1.0, 0.0).astype(BF)
    ones_high = jnp.where(lane < 64, 0.0, 1.0).astype(BF)

    def allowed(i, j):
        jj = (j + 64) % 64
        ok = (covis[i, jj] == 1) & (rank[jj] <= rank[i]) & (j >= 0) & (j < 64)
        return jnp.where(ok, 1.0, 0.0).astype(F32)

    def block(q, keys):
        sc = lax.dot_general(q, keys, (((1,), (1,)), ((), ())), preferred_element_type=F32)
        p = jnp.exp2(sc * EXP_SCALE).astype(BF)
        va = keys * ones_high + ones_low
        return dot(p, va)

    def pair(p):
        m = 2 - p // 3 - p // 5
        return p - 3 * (p // 3) - 2 * (p // 5), m

    def own_images():
        def step(n, _):
            done = [
                block(q_s[i].reshape(512, 128), kvr[i].reshape(1024, 128)) * allowed(base + i, base + i)
                for i in (2 * n, 2 * n + 1)
            ]
            acc[2 * n] = done[0]
            acc[2 * n + 1] = done[1]
            return 0

        lax.fori_loop(0, 2, step, 0)

    def row_pairs(n):
        done = []
        for p in (2 * n, 2 * n + 1):
            a, m = pair(p)
            b = m + 1
            ab = allowed(base + a, base + b)
            ba = allowed(base + b, base + a)
            q_of = jnp.where(ab > 0.5, a, b)
            r = block(q_s[q_of].reshape(512, 128), kvr[a + b - q_of].reshape(1024, 128))
            done.append((a, b, ab, ba, r))
        for a, b, ab, ba, r in done:
            acc[a] += r * ab
            acc[b] += r * ba

    def cross(d, pairs, first, count):
        done = []
        for a, m in pairs:
            i = column(a, d)
            j = (m - 3) * (1 - d) + (6 - m) * d
            keys = kvx[d, m, pl.ds(first, count)].reshape(256 * count, 128)
            done.append((i, block(q_s[i].reshape(512, 128), keys) * allowed(base + i, base + j)))
        for i, r in done:
            acc[i] += r

    near = t // 2
    far = 1 - near

    def near_pairs(n):
        cross(near, [pair(2 * n), pair(2 * n + 1)], 0, 4)

    w_local.wait()
    other_cols = pl.ds(pl.multiple_of((1 - c) * 128, 128), 128)
    rcopy(w, w3.at[:, :, other_cols], ws_sem.at[0], ws_sem.at[1], sib).wait_recv()
    project_row(4 + t)

    def z_step(k, _):
        def forward(h):
            def one(d, _):
                z = slot(k, d)

                @pl.when(arrives(k, d))
                def _():
                    rcopy(half_of(z, h), half_of(z, h), ag_send.at[z, h], ag_recv.at[z, h], sib).wait_recv()

                    @pl.when(passes_on(k, d))
                    def _():
                        pass_on(k, d, h, z).start()

                return 0

            lax.fori_loop(0, 2, one, 0)

        def spread_step(d, _):
            spread_keys(k - 1, d)
            return 0

        forward(0)

        @pl.when(k == 1)
        def _():
            row_arrived(4 + t)

        @pl.when(k > 1)
        def _():
            lax.fori_loop(0, 2, spread_step, 0)

        @pl.when((k == 5) | (k == 6))
        def _():
            row_pairs(2 * (k - 5))

        @pl.when(k == 7)
        def _():
            near_pairs(1)

        @pl.when(k == 3)
        def _():
            wo_local.wait()

        @pl.when(k == 4)
        def _():
            w_out_stage(wa_wait, wy_copy)

        @pl.when(k == 7)
        def _():
            for m in (1, 2, 3):
                wb_wait(m)
            wc.start()

        forward(1)

        @pl.when(k == 3)
        def _():
            for m in (1, 2, 3):
                wa_copy(m).start()

        @pl.when(k == 4)
        def _():
            w_out_stage(wy_wait, wb_copy)

        def project(d, _):
            z = slot(k, d)

            @pl.when(arrives(k, d))
            def _():
                @pl.when(is_row(k, d))
                def _():
                    project_row(z)

                @pl.when(is_cross(k, d))
                def _():
                    project_cross(z, d)

            return 0

        lax.fori_loop(0, 2, project, 0)

        @pl.when(k == 4)
        def _():
            for e in range(4):
                row_sib_wait(4 + e)
            own_images()

        @pl.when(k == 5)
        def _():
            row_pairs(1)

        @pl.when(k == 6)
        def _():
            for e in range(4):
                cross_sib_wait(8 * near + e, near)
            near_pairs(0)

        return 0

    lax.fori_loop(1, 8, z_step, 0)

    low64 = lax.broadcasted_iota(jnp.int32, (64, 128), 1) < 64
    head = t * 4 + y

    def f_copy(k, m):
        return rcopy(
            fsend.at[(y + k) % 4, (t + m) % 4], fin.at[head], f_send.at[k, m], f_recv.at[k, m], blk_dev(k, m)
        )

    def f_wait(k, m):
        other = ((t + 4 - m) % 4) * 4 + (y + 4 - k) % 4
        rcopy(fsend.at[0, 0], fin.at[other], f_send.at[k, m], f_recv.at[k, m], sib).wait_recv()

    def finish(a):
        i = column(a, far)
        for m in range(4):
            n = acc[i, m * 128:(m + 1) * 128, :]
            r = pltpu.roll(n, 64, 1)
            top = r[:64] / n[:64]
            bottom = n[64:] / r[64:]
            fsend[i, m] = jnp.where(low64, top, bottom).astype(BF)
        k = (i + 4 - y) % 4
        for m in range(1, 4):
            f_copy(k, m).start()

        @pl.when(k > 0)
        def _():
            f_copy(k, 0).start()

    near_pairs(2)
    finish(3)
    for e in range(3):
        cross_sib_wait(8 * far + 1 - far + e, far)
    cross(far, [pair(0), pair(1), pair(2)], 1 - far, 3)

    def last_spread(d, _):
        spread_keys(7, d)
        return 0

    lax.fori_loop(0, 2, last_spread, 0)
    cross(far, [pair(3), pair(4), pair(5)], 1 - far, 3)
    cross_sib_wait(11 * far, far)
    cross(far, [(2, 2), (1, 2), (1, 1)], 3 * far, 1)
    finish(2)
    finish(1)
    cross(far, [(0, 2), (0, 1), (0, 0)], 3 * far, 1)
    finish(0)
    fin[head] = fsend[y, t]
    order_f = [(k, m) for k in range(4) for m in range(4) if k or m]
    rcopy(wo.at[:, c], wo.at[:, 1 - c], wc_sem.at[0], wc_sem.at[1], sib).wait_recv()
    for k, m in order_f:
        f_wait(k, m)

    tops, bottoms = [], []
    for h in range(0, 16, 2):
        f0 = fin[h].astype(F32)
        f1 = fin[h + 1].astype(F32)
        tops.append(jnp.where(low64, f0, pltpu.roll(f1, 64, 1)).astype(BF))
        bottoms.append(jnp.where(low64, pltpu.roll(f0, 64, 1), f1).astype(BF))
    att = jnp.concatenate([jnp.concatenate(tops, axis=1), jnp.concatenate(bottoms, axis=1)], axis=0)
    out[...] = dot(att, wo[...].reshape(1024, 1024)).astype(BF)

    for d in (0, 1):

        @pl.when(passes_on(0, d))
        def _():
            for h in (0, 1):
                pass_on(0, d, h, 12 + d).wait_send()

    w_sib.wait_send()
    for m in (1, 2, 3):
        wa_copy(m).wait_send()
        wy_copy(m).wait_send()
        wb_copy(m).wait_send()
    wc.wait_send()

    def row_sent(z):
        for n in (1, 2, 3):
            row_copy(z, n).wait_send()
            yq_copy(z, n).wait_send()
        row_sib(z).wait_send()

    row_sent(4 + t)

    def sent(i, _):
        k = 1 + i // 2
        d = i % 2
        z = slot(k, d)

        @pl.when(arrives(k, d) & passes_on(k, d))
        def _():
            for h in (0, 1):
                pass_on(k, d, h, z).wait_send()

        @pl.when(is_row(k, d))
        def _():
            row_sent(z)

        @pl.when(is_cross(k, d))
        def _():
            @pl.when(column(y, d) >= 1)
            def _():
                for n in (1, 2, 3):
                    cross_copy(z, d, n).wait_send()

            cross_sib(z, d).wait_send()

        return 0

    lax.fori_loop(0, 14, sent, 0)
    for k, m in order_f:
        f_copy(k, m).wait_send()


def body(tokens, norm_gain, w_qkv, q_gain, k_gain, w_out, covis_mask, capture_rank):
    vm = pl.BlockSpec(memory_space=pltpu.VMEM)
    hbm = pl.BlockSpec(memory_space=pl.ANY)
    dma = pltpu.SemaphoreType.DMA
    result = pl.pallas_call(
        kernel,
        out_shape=jax.ShapeDtypeStruct((128, 1024), BF),
        in_specs=[hbm] * 8,
        out_specs=vm,
        scratch_shapes=[
            pltpu.VMEM((128, 1024), BF),
            pltpu.VMEM((1, 1024), F32),
            pltpu.VMEM((1, 64), F32),
            pltpu.VMEM((1, 64), F32),
            pltpu.SMEM((64, 64), jnp.int32),
            pltpu.SMEM((64,), jnp.int32),
            pltpu.VMEM((12, 128, 1024), BF),
            pltpu.VMEM((3, 1024, 256), BF),
            pltpu.VMEM((256, 256), BF),
            pltpu.VMEM((4, 4, 128, 128), BF),
            pltpu.VMEM((12, 4, 128, 128), BF),
            pltpu.VMEM((4, 4, 128, 128), BF),
            pltpu.VMEM((4, 4, 2, 128, 128), BF),
            pltpu.VMEM((2, 3, 4, 2, 128, 128), BF),
            pltpu.VMEM((4, 512, 128), F32),
            pltpu.VMEM((4, 2, 128, 1024), BF),
            pltpu.VMEM((16, 64, 128), BF),
            pltpu.VMEM((4, 4, 64, 128), BF),
            dma((8,)), dma((2,)), dma((14, 2)), dma((12, 2)),
            dma((4, 4)), dma((4, 4)), dma((12, 4)), dma((12, 4)), dma((12,)), dma((12,)),
            dma((4,)), dma((4,)), dma((4,)), dma((4,)), dma((4,)), dma((4,)), dma((2,)), dma((4, 4)), dma((4, 4)),
        ],
        compiler_params=pltpu.CompilerParams(
            collective_id=0, has_side_effects=True, vmem_limit_bytes=60 * 1024 * 1024
        ),
        cost_estimate=pl.CostEstimate(flops=10_000_000_000, bytes_accessed=4_000_000, transcendentals=15_000_000),
    )(
        tokens[0],
        norm_gain.reshape(1, 1024),
        jnp.transpose(w_qkv, (1, 0, 2)),
        q_gain.reshape(1, 64),
        k_gain.reshape(1, 64),
        w_out,
        covis_mask,
        capture_rank,
    )
    return result[None]


def solution(mesh):
    placed = (
        P("group", "slab", None),
        P(),
        P(None, None, "slab"),
        P(),
        P(),
        P("slab", None),
        P(),
        P(),
    )
    return jax.shard_map(
        body, mesh=mesh, in_specs=placed, out_specs=P("group", "slab", None), check_vma=False
    )
```

```python
import functools
import math

import jax
import jax.numpy as jnp
from jax import lax
from jax.experimental import pallas as pl
from jax.experimental.pallas import tpu as pltpu
from jax.sharding import PartitionSpec as P

MESH = pl.DeviceIdType.MESH
BF = jnp.bfloat16
F32 = jnp.float32
EPS = 1e-06
EXP_SCALE = 0.125 * math.log2(math.e)


def dot(a, b):
    return jnp.dot(a, b, preferred_element_type=F32)


def kernel(
    tok_h, ngain_h, w, qgain_h, kgain_h, w_out, covis_h, rank_h, out,
    tok, ngain, qgain, kgain, covis, rank, xg, w3, emat, stq, stkv, q_s, kvr, kvx, acc, wo, fin, fsend,
    loc_sem, ws_sem, ag_send, ag_recv, yq_send, yq_recv, yk_send, yk_recv, sib_send, sib_recv,
    wa_send, wa_recv, wy_send, wy_recv, wb_send, wb_recv, wc_sem, f_send, f_recv,
):
    g = lax.axis_index("group")
    s = lax.axis_index("slab")
    y = g % 4
    base = (g // 4) * 4
    x = g // 16
    zy = g % 16
    t = s // 2
    c = s % 2
    sib = (g, t * 2 + 1 - c)

    def y_dev(k):
        return (base + (y + k) % 4, s)

    def blk_dev(k, m):
        return (base + (y + k) % 4, ((t + m) % 4) * 2 + c)

    def x_dev(k):
        return (((x + k) % 4) * 16 + zy, s)

    def rcopy(src, dst, ss, rs, dev):
        return pltpu.make_async_remote_copy(
            src_ref=src, dst_ref=dst, send_sem=ss, recv_sem=rs, device_id=dev, device_id_type=MESH
        )

    def reach(d):
        return t * (1 - d) + (3 - t) * d

    def column(a, d):
        return a * (1 - d) + (3 - a) * d

    def slot(k, d):
        return 4 + t + (2 * d - 1) * k

    def next_dev(d):
        sign = 2 * d - 1
        edge = reach(d) // 3
        return ((g + 64 - 4 * sign * edge) % 64, s - 2 * sign + 8 * sign * edge)

    loads = [
        pltpu.make_async_copy(src, dst, loc_sem.at[2 + i])
        for i, (src, dst) in enumerate(
            [(tok_h, tok), (ngain_h, ngain), (qgain_h, qgain), (kgain_h, kgain), (covis_h, covis), (rank_h, rank)]
        )
    ]
    for copy in loads:
        copy.start()

    barrier = pltpu.get_barrier_semaphore()
    partners = [blk_dev(0, m) for m in (1, 2, 3)]
    partners += [((g + 60 + 8 * (t // 2)) % 64, (3 - t) * 2 + c), sib]
    partners += [y_dev(k) for k in (1, 2, 3)] + [x_dev(k) for k in (1, 2, 3)]
    for dev in partners:
        pl.semaphore_signal(barrier, inc=1, device_id=dev, device_id_type=MESH)

    own_cols = pl.ds(pl.multiple_of(c * 128, 128), 128)
    w_local = pltpu.make_async_copy(w, w3.at[:, :, own_cols], loc_sem.at[0])
    w_local.start()
    quarter = pl.ds(pl.multiple_of(x * 32, 32), 32)

    def part(a):
        return pl.ds(pl.multiple_of(a * 256, 256), 256)

    wo_local = pltpu.make_async_copy(
        w_out.at[quarter, part(y)], wo.at[t, c, quarter, part(y)], loc_sem.at[1]
    )
    wo_local.start()

    loads[0].wait()
    loads[1].wait()
    v = tok[...].astype(F32)
    centred = v - jnp.mean(v, axis=-1, keepdims=True)
    spread = jnp.mean(centred * centred, axis=-1, keepdims=True)
    xg[4 + t] = (centred * lax.rsqrt(spread + EPS) * ngain[...]).astype(BF)

    ri = lax.broadcasted_iota(jnp.int32, (256, 256), 0) // 64
    ci = lax.broadcasted_iota(jnp.int32, (256, 256), 1) // 64
    emat[...] = jnp.where(ri == ci, 1.0 / 64, 0.0).astype(BF)

    pl.semaphore_wait(barrier, len(partners))

    def half_of(z, h):
        return xg.at[z, pl.ds(pl.multiple_of(64 * h, 64), 64)]

    def pass_on(k, d, h, sem):
        here = slot(k, d)
        there = here + 4 * (2 * d - 1) * (reach(d) // 3)
        return rcopy(half_of(here, h), half_of(there, h), ag_send.at[sem, h], ag_recv.at[there, h], next_dev(d))

    def passes_on(k, d):
        return (reach(d) < 3) | ((k <= reach(d)) & (column(y, d) >= 1))

    def arrives(k, d):
        return (k <= reach(d)) | ((k <= reach(d) + 4) & (column(y, d) >= 1))

    for d in (0, 1):

        @pl.when(passes_on(0, d))
        def _():
            for h in (0, 1):
                pass_on(0, d, h, 12 + d).start()

    def wa_copy(m):
        piece = wo.at[t, c, quarter, part(y)]
        return rcopy(piece, piece, wa_send.at[m], wa_recv.at[m], (g, ((t + m) % 4) * 2 + c))

    def wy_copy(m):
        piece = wo.at[:, c, quarter, part(y)]
        return rcopy(piece, piece, wy_send.at[m], wy_recv.at[m], y_dev(m))

    def wb_copy(m):
        piece = wo.at[:, c, quarter]
        return rcopy(piece, piece, wb_send.at[m], wb_recv.at[m], x_dev(m))

    wc = rcopy(wo.at[:, c], wo.at[:, c], wc_sem.at[0], wc_sem.at[1], sib)

    def wa_wait(m):
        piece = wo.at[t, c, quarter, part(y)]
        rcopy(piece, wo.at[(t + 4 - m) % 4, c, quarter, part(y)], wa_send.at[m], wa_recv.at[m], sib).wait_recv()

    def wy_wait(m):
        piece = wo.at[:, c, quarter, part(y)]
        rcopy(piece, wo.at[:, c, quarter, part((y + 4 - m) % 4)], wy_send.at[m], wy_recv.at[m], sib).wait_recv()

    def wb_wait(m):
        other = pl.ds(pl.multiple_of((x + 4 - m) % 4 * 32, 32), 32)
        rcopy(wo.at[:, c, quarter], wo.at[:, c, other], wb_send.at[m], wb_recv.at[m], sib).wait_recv()

    def w_out_stage(wait, start):
        for m in (1, 2, 3):
            wait(m)
        for m in (1, 2, 3):
            start(m).start()

    wo_local.wait()
    for m in (1, 2, 3):
        wa_copy(m).start()

    w_sib = rcopy(w, w3.at[:, :, own_cols], ws_sem.at[0], ws_sem.at[1], sib)
    w_sib.start()
    for copy in loads[2:]:
        copy.wait()

    def group_mean(a):
        hi = a.astype(BF)
        lo = (a - hi.astype(F32)).astype(BF)
        return dot(hi, emat[...]) + dot(lo, emat[...])

    def head_norm(a, gain):
        b = a - group_mean(a)
        return b * lax.rsqrt(group_mean(b * b) + EPS) * gain

    qg = jnp.concatenate([qgain[...]] * 4, axis=1)
    kg = jnp.concatenate([kgain[...]] * 4, axis=1)
    low = lax.broadcasted_iota(jnp.int32, (128, 128), 1) < 64

    def yq_copy(z, k):
        return rcopy(stq.at[z - 4, (y + k) % 4], q_s.at[y, z - 4], yq_send.at[z - 4, k], yq_recv.at[z - 4, k], y_dev(k))

    def row_copy(z, k):
        return rcopy(
            stkv.at[z, (y + k) % 4], kvr.at[y, z - 4, c], yk_send.at[z, k], yk_recv.at[z, k], y_dev(k)
        )

    def cross_copy(z, d, k):
        return rcopy(
            stkv.at[z, (y + k) % 4], kvx.at[d, column(y, d) - 1, z % 4, c], yk_send.at[z, k], yk_recv.at[z, k], y_dev(k)
        )

    def yq_wait(z, k):
        rcopy(
            stq.at[0, 0], q_s.at[(y + 4 - k) % 4, z - 4], yq_send.at[z - 4, k], yq_recv.at[z - 4, k], sib
        ).wait_recv()

    def row_wait(z, k):
        rcopy(stkv.at[0, 0], kvr.at[(y + 4 - k) % 4, z - 4, c], yk_send.at[z, k], yk_recv.at[z, k], sib).wait_recv()

    def cross_wait(z, d, k):
        m = column((y + 4 - k) % 4, d) - 1
        rcopy(stkv.at[0, 0], kvx.at[d, m, z % 4, c], yk_send.at[z, k], yk_recv.at[z, k], sib).wait_recv()

    def project_keys(z):
        h = xg[z]
        kn = head_norm(dot(h, w3[1]), kg)
        vn = dot(h, w3[2])
        for a in range(2):
            cols = slice(128 * a, 128 * a + 128)
            k2, v2 = kn[:, cols], vn[:, cols]
            stkv[z, 2 * a] = jnp.where(low, k2, pltpu.roll(v2, 64, 1)).astype(BF)
            stkv[z, 2 * a + 1] = jnp.where(low, pltpu.roll(k2, 64, 1), v2).astype(BF)

    def project_queries(z):
        qn = head_norm(dot(xg[z], w3[0]), qg)
        for a in range(2):
            q2 = qn[:, 128 * a:128 * a + 128]
            stq[z - 4, 2 * a] = jnp.where(low, q2, 0.0).astype(BF)
            stq[z - 4, 2 * a + 1] = jnp.where(low, pltpu.roll(q2, 64, 1), 0.0).astype(BF)
        for k in (1, 2, 3):
            yq_copy(z, k).start()
        q_s[y, z - 4] = stq[z - 4, y]

    def project_row(z):
        project_keys(z)
        for k in (1, 2, 3):
            row_copy(z, k).start()
        kvr[y, z - 4, c] = stkv[z, y]
        project_queries(z)

    def project_cross(z, d):
        project_keys(z)
        for k in (1, 2, 3):
            cross_copy(z, d, k).start()
        kvx[d, column(y, d) - 1, z % 4, c] = stkv[z, y]

    def row_sib(z):
        return rcopy(kvr.at[:, z - 4, c], kvr.at[:, z - 4, c], sib_send.at[z], sib_recv.at[z], sib)

    def row_sib_wait(z):
        rcopy(kvr.at[:, z - 4, c], kvr.at[:, z - 4, 1 - c], sib_send.at[z], sib_recv.at[z], sib).wait_recv()

    def cross_sib(z, d):
        return rcopy(kvx.at[d, :, z % 4, c], kvx.at[d, :, z % 4, c], sib_send.at[z], sib_recv.at[z], sib)

    def cross_sib_wait(z, d):
        rcopy(kvx.at[d, :, z % 4, c], kvx.at[d, :, z % 4, 1 - c], sib_send.at[z], sib_recv.at[z], sib).wait_recv()

    def row_arrived(z):
        for k in (1, 2, 3):
            row_wait(z, k)
        row_sib(z).start()
        for k in (1, 2, 3):
            yq_wait(z, k)

    def is_row(k, d):
        return k <= reach(d)

    def is_cross(k, d):
        return (k > reach(d)) & (k <= reach(d) + 4)

    def spread_keys(k, d):
        z = slot(k, d)

        @pl.when(is_row(k, d))
        def _():
            row_arrived(z)

        @pl.when(is_cross(k, d))
        def _():
            for n in (1, 2, 3):

                @pl.when(column((y + 4 - n) % 4, d) >= 1)
                def _():
                    cross_wait(z, d, n)

            cross_sib(z, d).start()

    lane = lax.broadcasted_iota(jnp.int32, (1, 128), 1)
    ones_low = jnp.where(lane < 64, 1.0, 0.0).astype(BF)
    ones_high = jnp.where(lane < 64, 0.0, 1.0).astype(BF)

    def allowed(i, j):
        jj = (j + 64) % 64
        ok = (covis[i, jj] == 1) & (rank[jj] <= rank[i]) & (j >= 0) & (j < 64)
        return jnp.where(ok, 1.0, 0.0).astype(F32)

    def block(q, keys):
        sc = lax.dot_general(q, keys, (((1,), (1,)), ((), ())), preferred_element_type=F32)
        p = jnp.exp2(sc * EXP_SCALE).astype(BF)
        va = keys * ones_high + ones_low
        return dot(p, va)

    def pair(p):
        m = 2 - p // 3 - p // 5
        return p - 3 * (p // 3) - 2 * (p // 5), m

    def own_images():
        def step(n, _):
            done = [
                block(q_s[i].reshape(512, 128), kvr[i].reshape(1024, 128)) * allowed(base + i, base + i)
                for i in (2 * n, 2 * n + 1)
            ]
            acc[2 * n] = done[0]
            acc[2 * n + 1] = done[1]
            return 0

        lax.fori_loop(0, 2, step, 0)

    def row_pairs(n):
        done = []
        for p in (2 * n, 2 * n + 1):
            a, m = pair(p)
            b = m + 1
            ab = allowed(base + a, base + b)
            ba = allowed(base + b, base + a)
            q_of = jnp.where(ab > 0.5, a, b)
            r = block(q_s[q_of].reshape(512, 128), kvr[a + b - q_of].reshape(1024, 128))
            done.append((a, b, ab, ba, r))
        for a, b, ab, ba, r in done:
            acc[a] += r * ab
            acc[b] += r * ba

    def cross(d, pairs, first, count):
        done = []
        for a, m in pairs:
            i = column(a, d)
            j = (m - 3) * (1 - d) + (6 - m) * d
            keys = kvx[d, m, pl.ds(first, count)].reshape(256 * count, 128)
            done.append((i, block(q_s[i].reshape(512, 128), keys) * allowed(base + i, base + j)))
        for i, r in done:
            acc[i] += r

    near = t // 2
    far = 1 - near

    def near_pairs(n):
        cross(near, [pair(2 * n), pair(2 * n + 1)], 0, 4)

    w_local.wait()
    other_cols = pl.ds(pl.multiple_of((1 - c) * 128, 128), 128)
    rcopy(w, w3.at[:, :, other_cols], ws_sem.at[0], ws_sem.at[1], sib).wait_recv()
    project_row(4 + t)

    def z_step(k, _):
        def forward(h):
            def one(d, _):
                z = slot(k, d)

                @pl.when(arrives(k, d))
                def _():
                    rcopy(half_of(z, h), half_of(z, h), ag_send.at[z, h], ag_recv.at[z, h], sib).wait_recv()

                    @pl.when(passes_on(k, d))
                    def _():
                        pass_on(k, d, h, z).start()

                return 0

            lax.fori_loop(0, 2, one, 0)

        def spread_step(d, _):
            spread_keys(k - 1, d)
            return 0

        forward(0)

        @pl.when(k == 1)
        def _():
            row_arrived(4 + t)

        @pl.when(k > 1)
        def _():
            lax.fori_loop(0, 2, spread_step, 0)

        @pl.when((k == 5) | (k == 6))
        def _():
            row_pairs(2 * (k - 5))

        @pl.when(k == 7)
        def _():
            near_pairs(1)

        forward(1)

        @pl.when(k == 2)
        def _():
            w_out_stage(wa_wait, wy_copy)

        @pl.when(k == 3)
        def _():
            w_out_stage(wy_wait, wb_copy)

        @pl.when(k == 6)
        def _():
            for m in (1, 2, 3):
                wb_wait(m)
            wc.start()

        def project(d, _):
            z = slot(k, d)

            @pl.when(arrives(k, d))
            def _():
                @pl.when(is_row(k, d))
                def _():
                    project_row(z)

                @pl.when(is_cross(k, d))
                def _():
                    project_cross(z, d)

            return 0

        lax.fori_loop(0, 2, project, 0)

        @pl.when(k == 4)
        def _():
            for e in range(4):
                row_sib_wait(4 + e)
            own_images()

        @pl.when(k == 5)
        def _():
            row_pairs(1)

        @pl.when(k == 6)
        def _():
            for e in range(4):
                cross_sib_wait(8 * near + e, near)
            near_pairs(0)

        return 0

    lax.fori_loop(1, 8, z_step, 0)

    low64 = lax.broadcasted_iota(jnp.int32, (64, 128), 1) < 64
    head = t * 4 + y

    def f_copy(k, m):
        return rcopy(
            fsend.at[(y + k) % 4, (t + m) % 4], fin.at[head], f_send.at[k, m], f_recv.at[k, m], blk_dev(k, m)
        )

    def f_wait(k, m):
        other = ((t + 4 - m) % 4) * 4 + (y + 4 - k) % 4
        rcopy(fsend.at[0, 0], fin.at[other], f_send.at[k, m], f_recv.at[k, m], sib).wait_recv()

    def finish(a):
        i = column(a, far)
        for m in range(4):
            n = acc[i, m * 128:(m + 1) * 128, :]
            r = pltpu.roll(n, 64, 1)
            top = r[:64] / n[:64]
            bottom = n[64:] / r[64:]
            fsend[i, m] = jnp.where(low64, top, bottom).astype(BF)
        k = (i + 4 - y) % 4
        for m in range(1, 4):
            f_copy(k, m).start()

        @pl.when(k > 0)
        def _():
            f_copy(k, 0).start()

    near_pairs(2)
    finish(3)
    for e in range(3):
        cross_sib_wait(8 * far + 1 - far + e, far)
    cross(far, [pair(0), pair(1), pair(2)], 1 - far, 3)

    def last_spread(d, _):
        spread_keys(7, d)
        return 0

    lax.fori_loop(0, 2, last_spread, 0)
    cross(far, [pair(3), pair(4), pair(5)], 1 - far, 3)
    cross_sib_wait(11 * far, far)
    cross(far, [(2, 2), (1, 2), (1, 1)], 3 * far, 1)
    finish(2)
    finish(1)
    cross(far, [(0, 2), (0, 1), (0, 0)], 3 * far, 1)
    finish(0)
    fin[head] = fsend[y, t]
    order_f = [(k, m) for k in range(4) for m in range(4) if k or m]
    rcopy(wo.at[:, c], wo.at[:, 1 - c], wc_sem.at[0], wc_sem.at[1], sib).wait_recv()
    for k, m in order_f:
        f_wait(k, m)

    tops, bottoms = [], []
    for h in range(0, 16, 2):
        f0 = fin[h].astype(F32)
        f1 = fin[h + 1].astype(F32)
        tops.append(jnp.where(low64, f0, pltpu.roll(f1, 64, 1)).astype(BF))
        bottoms.append(jnp.where(low64, pltpu.roll(f0, 64, 1), f1).astype(BF))
    att = jnp.concatenate([jnp.concatenate(tops, axis=1), jnp.concatenate(bottoms, axis=1)], axis=0)
    out[...] = dot(att, wo[...].reshape(1024, 1024)).astype(BF)

    for d in (0, 1):

        @pl.when(passes_on(0, d))
        def _():
            for h in (0, 1):
                pass_on(0, d, h, 12 + d).wait_send()

    w_sib.wait_send()
    for m in (1, 2, 3):
        wa_copy(m).wait_send()
        wy_copy(m).wait_send()
        wb_copy(m).wait_send()
    wc.wait_send()

    def row_sent(z):
        for n in (1, 2, 3):
            row_copy(z, n).wait_send()
            yq_copy(z, n).wait_send()
        row_sib(z).wait_send()

    row_sent(4 + t)

    def sent(i, _):
        k = 1 + i // 2
        d = i % 2
        z = slot(k, d)

        @pl.when(arrives(k, d) & passes_on(k, d))
        def _():
            for h in (0, 1):
                pass_on(k, d, h, z).wait_send()

        @pl.when(is_row(k, d))
        def _():
            row_sent(z)

        @pl.when(is_cross(k, d))
        def _():
            @pl.when(column(y, d) >= 1)
            def _():
                for n in (1, 2, 3):
                    cross_copy(z, d, n).wait_send()

            cross_sib(z, d).wait_send()

        return 0

    lax.fori_loop(0, 14, sent, 0)
    for k, m in order_f:
        f_copy(k, m).wait_send()


def body(tokens, norm_gain, w_qkv, q_gain, k_gain, w_out, covis_mask, capture_rank):
    vm = pl.BlockSpec(memory_space=pltpu.VMEM)
    hbm = pl.BlockSpec(memory_space=pl.ANY)
    dma = pltpu.SemaphoreType.DMA
    result = pl.pallas_call(
        kernel,
        out_shape=jax.ShapeDtypeStruct((128, 1024), BF),
        in_specs=[hbm] * 8,
        out_specs=vm,
        scratch_shapes=[
            pltpu.VMEM((128, 1024), BF),
            pltpu.VMEM((1, 1024), F32),
            pltpu.VMEM((1, 64), F32),
            pltpu.VMEM((1, 64), F32),
            pltpu.SMEM((64, 64), jnp.int32),
            pltpu.SMEM((64,), jnp.int32),
            pltpu.VMEM((12, 128, 1024), BF),
            pltpu.VMEM((3, 1024, 256), BF),
            pltpu.VMEM((256, 256), BF),
            pltpu.VMEM((4, 4, 128, 128), BF),
            pltpu.VMEM((12, 4, 128, 128), BF),
            pltpu.VMEM((4, 4, 128, 128), BF),
            pltpu.VMEM((4, 4, 2, 128, 128), BF),
            pltpu.VMEM((2, 3, 4, 2, 128, 128), BF),
            pltpu.VMEM((4, 512, 128), F32),
            pltpu.VMEM((4, 2, 128, 1024), BF),
            pltpu.VMEM((16, 64, 128), BF),
            pltpu.VMEM((4, 4, 64, 128), BF),
            dma((8,)), dma((2,)), dma((14, 2)), dma((12, 2)),
            dma((4, 4)), dma((4, 4)), dma((12, 4)), dma((12, 4)), dma((12,)), dma((12,)),
            dma((4,)), dma((4,)), dma((4,)), dma((4,)), dma((4,)), dma((4,)), dma((2,)), dma((4, 4)), dma((4, 4)),
        ],
        compiler_params=pltpu.CompilerParams(
            collective_id=0, has_side_effects=True, vmem_limit_bytes=60 * 1024 * 1024
        ),
        cost_estimate=pl.CostEstimate(flops=10_000_000_000, bytes_accessed=4_000_000, transcendentals=15_000_000),
    )(
        tokens[0],
        norm_gain.reshape(1, 1024),
        jnp.transpose(w_qkv, (1, 0, 2)),
        q_gain.reshape(1, 64),
        k_gain.reshape(1, 64),
        w_out,
        covis_mask,
        capture_rank,
    )
    return result[None]


def solution(mesh):
    placed = (
        P("group", "slab", None),
        P(),
        P(None, None, "slab"),
        P(),
        P(),
        P("slab", None),
        P(),
        P(),
    )
    return jax.shard_map(
        body, mesh=mesh, in_specs=placed, out_specs=P("group", "slab", None), check_vma=False
    )
```

```python
import functools
import math

import jax
import jax.numpy as jnp
from jax import lax
from jax.experimental import pallas as pl
from jax.experimental.pallas import tpu as pltpu
from jax.sharding import PartitionSpec as P

MESH = pl.DeviceIdType.MESH
BF = jnp.bfloat16
F32 = jnp.float32
EPS = 1e-06
EXP_SCALE = 0.125 * math.log2(math.e)


def dot(a, b):
    return jnp.dot(a, b, preferred_element_type=F32)


def kernel(
    tok_h, ngain_h, w, qgain_h, kgain_h, w_out, covis_h, rank_h, out,
    tok, ngain, qgain, kgain, covis, rank, xg, w3, emat, stq, stkv, q_s, kvr, kvx, acc, wo, fin, fsend,
    loc_sem, ws_sem, ag_send, ag_recv, yq_send, yq_recv, yk_send, yk_recv, sib_send, sib_recv,
    wa_send, wa_recv, wy_send, wy_recv, wb_send, wb_recv, wc_sem, f_send, f_recv,
):
    g = lax.axis_index("group")
    s = lax.axis_index("slab")
    y = g % 4
    base = (g // 4) * 4
    x = g // 16
    zy = g % 16
    t = s // 2
    c = s % 2
    sib = (g, t * 2 + 1 - c)

    def y_dev(k):
        return (base + (y + k) % 4, s)

    def blk_dev(k, m):
        return (base + (y + k) % 4, ((t + m) % 4) * 2 + c)

    def x_dev(k):
        return (((x + k) % 4) * 16 + zy, s)

    def rcopy(src, dst, ss, rs, dev):
        return pltpu.make_async_remote_copy(
            src_ref=src, dst_ref=dst, send_sem=ss, recv_sem=rs, device_id=dev, device_id_type=MESH
        )

    def reach(d):
        return t * (1 - d) + (3 - t) * d

    def column(a, d):
        return a * (1 - d) + (3 - a) * d

    def slot(k, d):
        return 4 + t + (2 * d - 1) * k

    def next_dev(d):
        sign = 2 * d - 1
        edge = reach(d) // 3
        return ((g + 64 - 4 * sign * edge) % 64, s - 2 * sign + 8 * sign * edge)

    loads = [
        pltpu.make_async_copy(src, dst, loc_sem.at[2 + i])
        for i, (src, dst) in enumerate(
            [(tok_h, tok), (ngain_h, ngain), (qgain_h, qgain), (kgain_h, kgain), (covis_h, covis), (rank_h, rank)]
        )
    ]
    for copy in loads:
        copy.start()

    barrier = pltpu.get_barrier_semaphore()
    partners = [blk_dev(0, m) for m in (1, 2, 3)]
    partners += [((g + 60 + 8 * (t // 2)) % 64, (3 - t) * 2 + c), sib]
    partners += [y_dev(k) for k in (1, 2, 3)] + [x_dev(k) for k in (1, 2, 3)]
    for dev in partners:
        pl.semaphore_signal(barrier, inc=1, device_id=dev, device_id_type=MESH)

    own_cols = pl.ds(pl.multiple_of(c * 128, 128), 128)
    w_local = pltpu.make_async_copy(w, w3.at[:, :, own_cols], loc_sem.at[0])
    w_local.start()
    quarter = pl.ds(pl.multiple_of(x * 32, 32), 32)

    def part(a):
        return pl.ds(pl.multiple_of(a * 256, 256), 256)

    wo_local = pltpu.make_async_copy(
        w_out.at[quarter, part(y)], wo.at[t, c, quarter, part(y)], loc_sem.at[1]
    )
    wo_local.start()

    loads[0].wait()
    loads[1].wait()
    v = tok[...].astype(F32)
    centred = v - jnp.mean(v, axis=-1, keepdims=True)
    spread = jnp.mean(centred * centred, axis=-1, keepdims=True)
    xg[4 + t] = (centred * lax.rsqrt(spread + EPS) * ngain[...]).astype(BF)

    ri = lax.broadcasted_iota(jnp.int32, (256, 256), 0) // 64
    ci = lax.broadcasted_iota(jnp.int32, (256, 256), 1) // 64
    emat[...] = jnp.where(ri == ci, 1.0 / 64, 0.0).astype(BF)

    pl.semaphore_wait(barrier, len(partners))

    def half_of(z, h):
        return xg.at[z, pl.ds(pl.multiple_of(64 * h, 64), 64)]

    def pass_on(k, d, h, sem):
        here = slot(k, d)
        there = here + 4 * (2 * d - 1) * (reach(d) // 3)
        return rcopy(half_of(here, h), half_of(there, h), ag_send.at[sem, h], ag_recv.at[there, h], next_dev(d))

    def passes_on(k, d):
        return (reach(d) < 3) | ((k <= reach(d)) & (column(y, d) >= 1))

    def arrives(k, d):
        return (k <= reach(d)) | ((k <= reach(d) + 4) & (column(y, d) >= 1))

    for d in (0, 1):

        @pl.when(passes_on(0, d))
        def _():
            for h in (0, 1):
                pass_on(0, d, h, 12 + d).start()

    def wa_copy(m):
        piece = wo.at[t, c, quarter, part(y)]
        return rcopy(piece, piece, wa_send.at[m], wa_recv.at[m], (g, ((t + m) % 4) * 2 + c))

    def wy_copy(m):
        piece = wo.at[:, c, quarter, part(y)]
        return rcopy(piece, piece, wy_send.at[m], wy_recv.at[m], y_dev(m))

    def wb_copy(m):
        piece = wo.at[:, c, quarter]
        return rcopy(piece, piece, wb_send.at[m], wb_recv.at[m], x_dev(m))

    wc = rcopy(wo.at[:, c], wo.at[:, c], wc_sem.at[0], wc_sem.at[1], sib)

    def wa_wait(m):
        piece = wo.at[t, c, quarter, part(y)]
        rcopy(piece, wo.at[(t + 4 - m) % 4, c, quarter, part(y)], wa_send.at[m], wa_recv.at[m], sib).wait_recv()

    def wy_wait(m):
        piece = wo.at[:, c, quarter, part(y)]
        rcopy(piece, wo.at[:, c, quarter, part((y + 4 - m) % 4)], wy_send.at[m], wy_recv.at[m], sib).wait_recv()

    def wb_wait(m):
        other = pl.ds(pl.multiple_of((x + 4 - m) % 4 * 32, 32), 32)
        rcopy(wo.at[:, c, quarter], wo.at[:, c, other], wb_send.at[m], wb_recv.at[m], sib).wait_recv()

    def w_out_stage(wait, start):
        for m in (1, 2, 3):
            wait(m)
        for m in (1, 2, 3):
            start(m).start()

    wo_local.wait()
    for m in (1, 2, 3):
        wa_copy(m).start()

    w_sib = rcopy(w, w3.at[:, :, own_cols], ws_sem.at[0], ws_sem.at[1], sib)
    w_sib.start()
    for copy in loads[2:]:
        copy.wait()

    def group_mean(a):
        hi = a.astype(BF)
        lo = (a - hi.astype(F32)).astype(BF)
        return dot(hi, emat[...]) + dot(lo, emat[...])

    def head_norm(a, gain):
        b = a - group_mean(a)
        return b * lax.rsqrt(group_mean(b * b) + EPS) * gain

    qg = jnp.concatenate([qgain[...]] * 4, axis=1)
    kg = jnp.concatenate([kgain[...]] * 4, axis=1)
    low = lax.broadcasted_iota(jnp.int32, (128, 128), 1) < 64

    def yq_copy(z, k):
        return rcopy(stq.at[z - 4, (y + k) % 4], q_s.at[y, z - 4], yq_send.at[z - 4, k], yq_recv.at[z - 4, k], y_dev(k))

    def row_copy(z, k):
        return rcopy(
            stkv.at[z, (y + k) % 4], kvr.at[y, z - 4, c], yk_send.at[z, k], yk_recv.at[z, k], y_dev(k)
        )

    def cross_copy(z, d, k):
        return rcopy(
            stkv.at[z, (y + k) % 4], kvx.at[d, column(y, d) - 1, z % 4, c], yk_send.at[z, k], yk_recv.at[z, k], y_dev(k)
        )

    def yq_wait(z, k):
        rcopy(
            stq.at[0, 0], q_s.at[(y + 4 - k) % 4, z - 4], yq_send.at[z - 4, k], yq_recv.at[z - 4, k], sib
        ).wait_recv()

    def row_wait(z, k):
        rcopy(stkv.at[0, 0], kvr.at[(y + 4 - k) % 4, z - 4, c], yk_send.at[z, k], yk_recv.at[z, k], sib).wait_recv()

    def cross_wait(z, d, k):
        m = column((y + 4 - k) % 4, d) - 1
        rcopy(stkv.at[0, 0], kvx.at[d, m, z % 4, c], yk_send.at[z, k], yk_recv.at[z, k], sib).wait_recv()

    def project_keys(z):
        h = xg[z]
        kn = head_norm(dot(h, w3[1]), kg)
        vn = dot(h, w3[2])
        for a in range(2):
            cols = slice(128 * a, 128 * a + 128)
            k2, v2 = kn[:, cols], vn[:, cols]
            stkv[z, 2 * a] = jnp.where(low, k2, pltpu.roll(v2, 64, 1)).astype(BF)
            stkv[z, 2 * a + 1] = jnp.where(low, pltpu.roll(k2, 64, 1), v2).astype(BF)

    def project_queries(z):
        qn = head_norm(dot(xg[z], w3[0]), qg)
        for a in range(2):
            q2 = qn[:, 128 * a:128 * a + 128]
            stq[z - 4, 2 * a] = jnp.where(low, q2, 0.0).astype(BF)
            stq[z - 4, 2 * a + 1] = jnp.where(low, pltpu.roll(q2, 64, 1), 0.0).astype(BF)
        for k in (1, 2, 3):
            yq_copy(z, k).start()
        q_s[y, z - 4] = stq[z - 4, y]

    def project_row(z):
        project_keys(z)
        for k in (1, 2, 3):
            row_copy(z, k).start()
        kvr[y, z - 4, c] = stkv[z, y]
        project_queries(z)

    def project_cross(z, d):
        project_keys(z)
        for k in (1, 2, 3):
            cross_copy(z, d, k).start()
        kvx[d, column(y, d) - 1, z % 4, c] = stkv[z, y]

    def row_sib(z):
        return rcopy(kvr.at[:, z - 4, c], kvr.at[:, z - 4, c], sib_send.at[z], sib_recv.at[z], sib)

    def row_sib_wait(z):
        rcopy(kvr.at[:, z - 4, c], kvr.at[:, z - 4, 1 - c], sib_send.at[z], sib_recv.at[z], sib).wait_recv()

    def cross_sib(z, d):
        return rcopy(kvx.at[d, :, z % 4, c], kvx.at[d, :, z % 4, c], sib_send.at[z], sib_recv.at[z], sib)

    def cross_sib_wait(z, d):
        rcopy(kvx.at[d, :, z % 4, c], kvx.at[d, :, z % 4, 1 - c], sib_send.at[z], sib_recv.at[z], sib).wait_recv()

    def row_arrived(z):
        for k in (1, 2, 3):
            row_wait(z, k)
        row_sib(z).start()
        for k in (1, 2, 3):
            yq_wait(z, k)

    def is_row(k, d):
        return k <= reach(d)

    def is_cross(k, d):
        return (k > reach(d)) & (k <= reach(d) + 4)

    def spread_keys(k, d):
        z = slot(k, d)

        @pl.when(is_row(k, d))
        def _():
            row_arrived(z)

        @pl.when(is_cross(k, d))
        def _():
            for n in (1, 2, 3):

                @pl.when(column((y + 4 - n) % 4, d) >= 1)
                def _():
                    cross_wait(z, d, n)

            cross_sib(z, d).start()

    lane = lax.broadcasted_iota(jnp.int32, (1, 128), 1)
    ones_low = jnp.where(lane < 64, 1.0, 0.0).astype(BF)
    ones_high = jnp.where(lane < 64, 0.0, 1.0).astype(BF)

    def allowed(i, j):
        jj = (j + 64) % 64
        ok = (covis[i, jj] == 1) & (rank[jj] <= rank[i]) & (j >= 0) & (j < 64)
        return jnp.where(ok, 1.0, 0.0).astype(F32)

    def block(q, keys):
        sc = lax.dot_general(q, keys, (((1,), (1,)), ((), ())), preferred_element_type=F32)
        p = jnp.exp2(sc * EXP_SCALE).astype(BF)
        va = keys * ones_high + ones_low
        return dot(p, va)

    def pair(p):
        m = 2 - p // 3 - p // 5
        return p - 3 * (p // 3) - 2 * (p // 5), m

    def own_images():
        def step(n, _):
            done = [
                block(q_s[i].reshape(512, 128), kvr[i].reshape(1024, 128)) * allowed(base + i, base + i)
                for i in (2 * n, 2 * n + 1)
            ]
            acc[2 * n] = done[0]
            acc[2 * n + 1] = done[1]
            return 0

        lax.fori_loop(0, 2, step, 0)

    def row_pairs(n):
        done = []
        for p in (2 * n, 2 * n + 1):
            a, m = pair(p)
            b = m + 1
            ab = allowed(base + a, base + b)
            ba = allowed(base + b, base + a)
            q_of = jnp.where(ab > 0.5, a, b)
            r = block(q_s[q_of].reshape(512, 128), kvr[a + b - q_of].reshape(1024, 128))
            done.append((a, b, ab, ba, r))
        for a, b, ab, ba, r in done:
            acc[a] += r * ab
            acc[b] += r * ba

    def cross(d, pairs, first, count):
        done = []
        for a, m in pairs:
            i = column(a, d)
            j = (m - 3) * (1 - d) + (6 - m) * d
            keys = kvx[d, m, pl.ds(first, count)].reshape(256 * count, 128)
            done.append((i, block(q_s[i].reshape(512, 128), keys) * allowed(base + i, base + j)))
        for i, r in done:
            acc[i] += r

    near = t // 2
    far = 1 - near

    def near_pairs(n):
        cross(near, [pair(2 * n), pair(2 * n + 1)], 0, 4)

    w_local.wait()
    other_cols = pl.ds(pl.multiple_of((1 - c) * 128, 128), 128)
    rcopy(w, w3.at[:, :, other_cols], ws_sem.at[0], ws_sem.at[1], sib).wait_recv()
    project_row(4 + t)

    def z_step(k, _):
        def forward(h):
            def one(d, _):
                z = slot(k, d)

                @pl.when(arrives(k, d))
                def _():
                    rcopy(half_of(z, h), half_of(z, h), ag_send.at[z, h], ag_recv.at[z, h], sib).wait_recv()

                    @pl.when(passes_on(k, d))
                    def _():
                        pass_on(k, d, h, z).start()

                return 0

            lax.fori_loop(0, 2, one, 0)

        def spread_step(d, _):
            spread_keys(k - 1, d)
            return 0

        forward(0)

        @pl.when(k == 1)
        def _():
            row_arrived(4 + t)

        @pl.when(k > 1)
        def _():
            lax.fori_loop(0, 2, spread_step, 0)

        forward(1)

        @pl.when(k == 2)
        def _():
            w_out_stage(wa_wait, wy_copy)

        @pl.when(k == 3)
        def _():
            w_out_stage(wy_wait, wb_copy)

        @pl.when(k == 6)
        def _():
            for m in (1, 2, 3):
                wb_wait(m)
            wc.start()

        def project(d, _):
            z = slot(k, d)

            @pl.when(arrives(k, d))
            def _():
                @pl.when(is_row(k, d))
                def _():
                    project_row(z)

                @pl.when(is_cross(k, d))
                def _():
                    project_cross(z, d)

            return 0

        lax.fori_loop(0, 2, project, 0)

        @pl.when(k == 4)
        def _():
            for e in range(4):
                row_sib_wait(4 + e)
            own_images()

        @pl.when((k == 5) | (k == 6))
        def _():
            row_pairs(2 * (k - 5))

        @pl.when(k == 5)
        def _():
            row_pairs(1)

        @pl.when(k == 6)
        def _():
            for e in range(4):
                cross_sib_wait(8 * near + e, near)
            near_pairs(0)

        @pl.when(k == 7)
        def _():
            near_pairs(1)

        return 0

    lax.fori_loop(1, 8, z_step, 0)

    low64 = lax.broadcasted_iota(jnp.int32, (64, 128), 1) < 64
    head = t * 4 + y

    def f_copy(k, m):
        return rcopy(
            fsend.at[(y + k) % 4, (t + m) % 4], fin.at[head], f_send.at[k, m], f_recv.at[k, m], blk_dev(k, m)
        )

    def f_wait(k, m):
        other = ((t + 4 - m) % 4) * 4 + (y + 4 - k) % 4
        rcopy(fsend.at[0, 0], fin.at[other], f_send.at[k, m], f_recv.at[k, m], sib).wait_recv()

    def finish(a):
        i = column(a, far)
        for m in range(4):
            n = acc[i, m * 128:(m + 1) * 128, :]
            r = pltpu.roll(n, 64, 1)
            top = r[:64] / n[:64]
            bottom = n[64:] / r[64:]
            fsend[i, m] = jnp.where(low64, top, bottom).astype(BF)
        k = (i + 4 - y) % 4
        for m in range(1, 4):
            f_copy(k, m).start()

        @pl.when(k > 0)
        def _():
            f_copy(k, 0).start()

    near_pairs(2)
    finish(3)
    for e in range(3):
        cross_sib_wait(8 * far + 1 - far + e, far)
    cross(far, [pair(0), pair(1), pair(2)], 1 - far, 3)

    def last_spread(d, _):
        spread_keys(7, d)
        return 0

    lax.fori_loop(0, 2, last_spread, 0)
    cross(far, [pair(3), pair(4), pair(5)], 1 - far, 3)
    cross_sib_wait(11 * far, far)
    cross(far, [(2, 2), (1, 2), (1, 1)], 3 * far, 1)
    finish(2)
    finish(1)
    cross(far, [(0, 2), (0, 1), (0, 0)], 3 * far, 1)
    finish(0)
    fin[head] = fsend[y, t]
    order_f = [(k, m) for k in range(4) for m in range(4) if k or m]
    rcopy(wo.at[:, c], wo.at[:, 1 - c], wc_sem.at[0], wc_sem.at[1], sib).wait_recv()
    for k, m in order_f:
        f_wait(k, m)

    tops, bottoms = [], []
    for h in range(0, 16, 2):
        f0 = fin[h].astype(F32)
        f1 = fin[h + 1].astype(F32)
        tops.append(jnp.where(low64, f0, pltpu.roll(f1, 64, 1)).astype(BF))
        bottoms.append(jnp.where(low64, pltpu.roll(f0, 64, 1), f1).astype(BF))
    att = jnp.concatenate([jnp.concatenate(tops, axis=1), jnp.concatenate(bottoms, axis=1)], axis=0)
    out[...] = dot(att, wo[...].reshape(1024, 1024)).astype(BF)

    for d in (0, 1):

        @pl.when(passes_on(0, d))
        def _():
            for h in (0, 1):
                pass_on(0, d, h, 12 + d).wait_send()

    w_sib.wait_send()
    for m in (1, 2, 3):
        wa_copy(m).wait_send()
        wy_copy(m).wait_send()
        wb_copy(m).wait_send()
    wc.wait_send()

    def row_sent(z):
        for n in (1, 2, 3):
            row_copy(z, n).wait_send()
            yq_copy(z, n).wait_send()
        row_sib(z).wait_send()

    row_sent(4 + t)

    def sent(i, _):
        k = 1 + i // 2
        d = i % 2
        z = slot(k, d)

        @pl.when(arrives(k, d) & passes_on(k, d))
        def _():
            for h in (0, 1):
                pass_on(k, d, h, z).wait_send()

        @pl.when(is_row(k, d))
        def _():
            row_sent(z)

        @pl.when(is_cross(k, d))
        def _():
            @pl.when(column(y, d) >= 1)
            def _():
                for n in (1, 2, 3):
                    cross_copy(z, d, n).wait_send()

            cross_sib(z, d).wait_send()

        return 0

    lax.fori_loop(0, 14, sent, 0)
    for k, m in order_f:
        f_copy(k, m).wait_send()


def body(tokens, norm_gain, w_qkv, q_gain, k_gain, w_out, covis_mask, capture_rank):
    vm = pl.BlockSpec(memory_space=pltpu.VMEM)
    hbm = pl.BlockSpec(memory_space=pl.ANY)
    dma = pltpu.SemaphoreType.DMA
    result = pl.pallas_call(
        kernel,
        out_shape=jax.ShapeDtypeStruct((128, 1024), BF),
        in_specs=[hbm] * 8,
        out_specs=vm,
        scratch_shapes=[
            pltpu.VMEM((128, 1024), BF),
            pltpu.VMEM((1, 1024), F32),
            pltpu.VMEM((1, 64), F32),
            pltpu.VMEM((1, 64), F32),
            pltpu.SMEM((64, 64), jnp.int32),
            pltpu.SMEM((64,), jnp.int32),
            pltpu.VMEM((12, 128, 1024), BF),
            pltpu.VMEM((3, 1024, 256), BF),
            pltpu.VMEM((256, 256), BF),
            pltpu.VMEM((4, 4, 128, 128), BF),
            pltpu.VMEM((12, 4, 128, 128), BF),
            pltpu.VMEM((4, 4, 128, 128), BF),
            pltpu.VMEM((4, 4, 2, 128, 128), BF),
            pltpu.VMEM((2, 3, 4, 2, 128, 128), BF),
            pltpu.VMEM((4, 512, 128), F32),
            pltpu.VMEM((4, 2, 128, 1024), BF),
            pltpu.VMEM((16, 64, 128), BF),
            pltpu.VMEM((4, 4, 64, 128), BF),
            dma((8,)), dma((2,)), dma((14, 2)), dma((12, 2)),
            dma((4, 4)), dma((4, 4)), dma((12, 4)), dma((12, 4)), dma((12,)), dma((12,)),
            dma((4,)), dma((4,)), dma((4,)), dma((4,)), dma((4,)), dma((4,)), dma((2,)), dma((4, 4)), dma((4, 4)),
        ],
        compiler_params=pltpu.CompilerParams(
            collective_id=0, has_side_effects=True, vmem_limit_bytes=60 * 1024 * 1024
        ),
        cost_estimate=pl.CostEstimate(flops=10_000_000_000, bytes_accessed=4_000_000, transcendentals=15_000_000),
    )(
        tokens[0],
        norm_gain.reshape(1, 1024),
        jnp.transpose(w_qkv, (1, 0, 2)),
        q_gain.reshape(1, 64),
        k_gain.reshape(1, 64),
        w_out,
        covis_mask,
        capture_rank,
    )
    return result[None]


def solution(mesh):
    placed = (
        P("group", "slab", None),
        P(),
        P(None, None, "slab"),
        P(),
        P(),
        P("slab", None),
        P(),
        P(),
    )
    return jax.shard_map(
        body, mesh=mesh, in_specs=placed, out_specs=P("group", "slab", None), check_vma=False
    )
```

```python
import functools
import math

import jax
import jax.numpy as jnp
from jax import lax
from jax.experimental import pallas as pl
from jax.experimental.pallas import tpu as pltpu
from jax.sharding import PartitionSpec as P

MESH = pl.DeviceIdType.MESH
BF = jnp.bfloat16
F32 = jnp.float32
EPS = 1e-06
EXP_SCALE = 0.125 * math.log2(math.e)


def dot(a, b):
    return jnp.dot(a, b, preferred_element_type=F32)


def kernel(
    tok_h, ngain_h, w, qgain_h, kgain_h, w_out, covis_h, rank_h, out,
    tok, ngain, qgain, kgain, covis, rank, xg, w3, emat, stq, stkv, q_s, kvr, kvx, acc, wo, fin, fsend,
    loc_sem, ws_sem, ag_send, ag_recv, yq_send, yq_recv, yk_send, yk_recv, sib_send, sib_recv,
    wa_send, wa_recv, wy_send, wy_recv, wb_send, wb_recv, wc_sem, f_send, f_recv,
):
    g = lax.axis_index("group")
    s = lax.axis_index("slab")
    y = g % 4
    base = (g // 4) * 4
    x = g // 16
    zy = g % 16
    t = s // 2
    c = s % 2
    sib = (g, t * 2 + 1 - c)

    def y_dev(k):
        return (base + (y + k) % 4, s)

    def blk_dev(k, m):
        return (base + (y + k) % 4, ((t + m) % 4) * 2 + c)

    def x_dev(k):
        return (((x + k) % 4) * 16 + zy, s)

    def rcopy(src, dst, ss, rs, dev):
        return pltpu.make_async_remote_copy(
            src_ref=src, dst_ref=dst, send_sem=ss, recv_sem=rs, device_id=dev, device_id_type=MESH
        )

    def reach(d):
        return t * (1 - d) + (3 - t) * d

    def column(a, d):
        return a * (1 - d) + (3 - a) * d

    def slot(k, d):
        return 4 + t + (2 * d - 1) * k

    def next_dev(d):
        sign = 2 * d - 1
        edge = reach(d) // 3
        return ((g + 64 - 4 * sign * edge) % 64, s - 2 * sign + 8 * sign * edge)

    loads = [
        pltpu.make_async_copy(src, dst, loc_sem.at[2 + i])
        for i, (src, dst) in enumerate(
            [(tok_h, tok), (ngain_h, ngain), (qgain_h, qgain), (kgain_h, kgain), (covis_h, covis), (rank_h, rank)]
        )
    ]
    for copy in loads:
        copy.start()

    barrier = pltpu.get_barrier_semaphore()
    partners = [blk_dev(0, m) for m in (1, 2, 3)]
    partners += [((g + 60 + 8 * (t // 2)) % 64, (3 - t) * 2 + c), sib]
    partners += [y_dev(k) for k in (1, 2, 3)] + [x_dev(k) for k in (1, 2, 3)]
    for dev in partners:
        pl.semaphore_signal(barrier, inc=1, device_id=dev, device_id_type=MESH)

    own_cols = pl.ds(pl.multiple_of(c * 128, 128), 128)
    w_local = pltpu.make_async_copy(w, w3.at[:, :, own_cols], loc_sem.at[0])
    w_local.start()
    quarter = pl.ds(pl.multiple_of(x * 32, 32), 32)

    def part(a):
        return pl.ds(pl.multiple_of(a * 256, 256), 256)

    wo_local = pltpu.make_async_copy(
        w_out.at[quarter, part(y)], wo.at[t, c, quarter, part(y)], loc_sem.at[1]
    )
    wo_local.start()

    loads[0].wait()
    loads[1].wait()
    v = tok[...].astype(F32)
    centred = v - jnp.mean(v, axis=-1, keepdims=True)
    spread = jnp.mean(centred * centred, axis=-1, keepdims=True)
    xg[4 + t] = (centred * lax.rsqrt(spread + EPS) * ngain[...]).astype(BF)

    ri = lax.broadcasted_iota(jnp.int32, (256, 256), 0) // 64
    ci = lax.broadcasted_iota(jnp.int32, (256, 256), 1) // 64
    emat[...] = jnp.where(ri == ci, 1.0 / 64, 0.0).astype(BF)

    pl.semaphore_wait(barrier, len(partners))

    def half_of(z, h):
        return xg.at[z, pl.ds(pl.multiple_of(64 * h, 64), 64)]

    def pass_on(k, d, h, sem):
        here = slot(k, d)
        there = here + 4 * (2 * d - 1) * (reach(d) // 3)
        return rcopy(half_of(here, h), half_of(there, h), ag_send.at[sem, h], ag_recv.at[there, h], next_dev(d))

    def passes_on(k, d):
        return (reach(d) < 3) | ((k <= reach(d)) & (column(y, d) >= 1))

    def arrives(k, d):
        return (k <= reach(d)) | ((k <= reach(d) + 4) & (column(y, d) >= 1))

    for d in (0, 1):

        @pl.when(passes_on(0, d))
        def _():
            for h in (0, 1):
                pass_on(0, d, h, 12 + d).start()

    def wa_copy(m):
        piece = wo.at[t, c, quarter, part(y)]
        return rcopy(piece, piece, wa_send.at[m], wa_recv.at[m], (g, ((t + m) % 4) * 2 + c))

    def wy_copy(m):
        piece = wo.at[:, c, quarter, part(y)]
        return rcopy(piece, piece, wy_send.at[m], wy_recv.at[m], y_dev(m))

    def wb_copy(m):
        piece = wo.at[:, c, quarter]
        return rcopy(piece, piece, wb_send.at[m], wb_recv.at[m], x_dev(m))

    wc = rcopy(wo.at[:, c], wo.at[:, c], wc_sem.at[0], wc_sem.at[1], sib)

    def wa_wait(m):
        piece = wo.at[t, c, quarter, part(y)]
        rcopy(piece, wo.at[(t + 4 - m) % 4, c, quarter, part(y)], wa_send.at[m], wa_recv.at[m], sib).wait_recv()

    def wy_wait(m):
        piece = wo.at[:, c, quarter, part(y)]
        rcopy(piece, wo.at[:, c, quarter, part((y + 4 - m) % 4)], wy_send.at[m], wy_recv.at[m], sib).wait_recv()

    def wb_wait(m):
        other = pl.ds(pl.multiple_of((x + 4 - m) % 4 * 32, 32), 32)
        rcopy(wo.at[:, c, quarter], wo.at[:, c, other], wb_send.at[m], wb_recv.at[m], sib).wait_recv()

    def w_out_stage(wait, start):
        for m in (1, 2, 3):
            wait(m)
        for m in (1, 2, 3):
            start(m).start()

    wo_local.wait()
    for m in (1, 2, 3):
        wa_copy(m).start()

    w_sib = rcopy(w, w3.at[:, :, own_cols], ws_sem.at[0], ws_sem.at[1], sib)
    w_sib.start()
    for copy in loads[2:]:
        copy.wait()

    def group_mean(a):
        hi = a.astype(BF)
        lo = (a - hi.astype(F32)).astype(BF)
        return dot(hi, emat[...]) + dot(lo, emat[...])

    def head_norm(a, gain):
        b = a - group_mean(a)
        return b * lax.rsqrt(group_mean(b * b) + EPS) * gain

    qg = jnp.concatenate([qgain[...]] * 4, axis=1)
    kg = jnp.concatenate([kgain[...]] * 4, axis=1)
    low = lax.broadcasted_iota(jnp.int32, (128, 128), 1) < 64

    def yq_copy(z, k):
        return rcopy(stq.at[z - 4, (y + k) % 4], q_s.at[y, z - 4], yq_send.at[z - 4, k], yq_recv.at[z - 4, k], y_dev(k))

    def row_copy(z, k):
        return rcopy(
            stkv.at[z, (y + k) % 4], kvr.at[y, z - 4, c], yk_send.at[z, k], yk_recv.at[z, k], y_dev(k)
        )

    def cross_copy(z, d, k):
        return rcopy(
            stkv.at[z, (y + k) % 4], kvx.at[d, column(y, d) - 1, z % 4, c], yk_send.at[z, k], yk_recv.at[z, k], y_dev(k)
        )

    def yq_wait(z, k):
        rcopy(
            stq.at[0, 0], q_s.at[(y + 4 - k) % 4, z - 4], yq_send.at[z - 4, k], yq_recv.at[z - 4, k], sib
        ).wait_recv()

    def row_wait(z, k):
        rcopy(stkv.at[0, 0], kvr.at[(y + 4 - k) % 4, z - 4, c], yk_send.at[z, k], yk_recv.at[z, k], sib).wait_recv()

    def cross_wait(z, d, k):
        m = column((y + 4 - k) % 4, d) - 1
        rcopy(stkv.at[0, 0], kvx.at[d, m, z % 4, c], yk_send.at[z, k], yk_recv.at[z, k], sib).wait_recv()

    def project_keys(z):
        h = xg[z]
        kn = head_norm(dot(h, w3[1]), kg)
        vn = dot(h, w3[2])
        for a in range(2):
            cols = slice(128 * a, 128 * a + 128)
            k2, v2 = kn[:, cols], vn[:, cols]
            stkv[z, 2 * a] = jnp.where(low, k2, pltpu.roll(v2, 64, 1)).astype(BF)
            stkv[z, 2 * a + 1] = jnp.where(low, pltpu.roll(k2, 64, 1), v2).astype(BF)

    def project_queries(z):
        qn = head_norm(dot(xg[z], w3[0]), qg)
        for a in range(2):
            q2 = qn[:, 128 * a:128 * a + 128]
            stq[z - 4, 2 * a] = jnp.where(low, q2, 0.0).astype(BF)
            stq[z - 4, 2 * a + 1] = jnp.where(low, pltpu.roll(q2, 64, 1), 0.0).astype(BF)
        for k in (1, 2, 3):
            yq_copy(z, k).start()
        q_s[y, z - 4] = stq[z - 4, y]

    def project_row(z):
        project_keys(z)
        for k in (1, 2, 3):
            row_copy(z, k).start()
        kvr[y, z - 4, c] = stkv[z, y]
        project_queries(z)

    def project_cross(z, d):
        project_keys(z)
        for k in (1, 2, 3):
            cross_copy(z, d, k).start()
        kvx[d, column(y, d) - 1, z % 4, c] = stkv[z, y]

    def row_sib(z):
        return rcopy(kvr.at[:, z - 4, c], kvr.at[:, z - 4, c], sib_send.at[z], sib_recv.at[z], sib)

    def row_sib_wait(z):
        rcopy(kvr.at[:, z - 4, c], kvr.at[:, z - 4, 1 - c], sib_send.at[z], sib_recv.at[z], sib).wait_recv()

    def cross_sib(z, d):
        return rcopy(kvx.at[d, :, z % 4, c], kvx.at[d, :, z % 4, c], sib_send.at[z], sib_recv.at[z], sib)

    def cross_sib_wait(z, d):
        rcopy(kvx.at[d, :, z % 4, c], kvx.at[d, :, z % 4, 1 - c], sib_send.at[z], sib_recv.at[z], sib).wait_recv()

    def row_arrived(z):
        for k in (1, 2, 3):
            row_wait(z, k)
        row_sib(z).start()
        for k in (1, 2, 3):
            yq_wait(z, k)

    def is_row(k, d):
        return k <= reach(d)

    def is_cross(k, d):
        return (k > reach(d)) & (k <= reach(d) + 4)

    def spread_keys(k, d):
        z = slot(k, d)

        @pl.when(is_row(k, d))
        def _():
            row_arrived(z)

        @pl.when(is_cross(k, d))
        def _():
            for n in (1, 2, 3):

                @pl.when(column((y + 4 - n) % 4, d) >= 1)
                def _():
                    cross_wait(z, d, n)

            cross_sib(z, d).start()

    lane = lax.broadcasted_iota(jnp.int32, (1, 128), 1)
    ones_low = jnp.where(lane < 64, 1.0, 0.0).astype(BF)
    ones_high = jnp.where(lane < 64, 0.0, 1.0).astype(BF)

    def allowed(i, j):
        jj = (j + 64) % 64
        ok = (covis[i, jj] == 1) & (rank[jj] <= rank[i]) & (j >= 0) & (j < 64)
        return jnp.where(ok, 1.0, 0.0).astype(F32)

    def block(q, keys):
        sc = lax.dot_general(q, keys, (((1,), (1,)), ((), ())), preferred_element_type=F32)
        p = jnp.exp2(sc * EXP_SCALE).astype(BF)
        va = keys * ones_high + ones_low
        return dot(p, va)

    def pair(p):
        m = 2 - p // 3 - p // 5
        return p - 3 * (p // 3) - 2 * (p // 5), m

    def own_images():
        def step(n, _):
            done = [
                block(q_s[i].reshape(512, 128), kvr[i].reshape(1024, 128)) * allowed(base + i, base + i)
                for i in (2 * n, 2 * n + 1)
            ]
            acc[2 * n] = done[0]
            acc[2 * n + 1] = done[1]
            return 0

        lax.fori_loop(0, 2, step, 0)

    def row_pairs(n):
        done = []
        for p in (2 * n, 2 * n + 1):
            a, m = pair(p)
            b = m + 1
            ab = allowed(base + a, base + b)
            ba = allowed(base + b, base + a)
            q_of = jnp.where(ab > 0.5, a, b)
            r = block(q_s[q_of].reshape(512, 128), kvr[a + b - q_of].reshape(1024, 128))
            done.append((a, b, ab, ba, r))
        for a, b, ab, ba, r in done:
            acc[a] += r * ab
            acc[b] += r * ba

    def cross(d, pairs, first, count):
        done = []
        for a, m in pairs:
            i = column(a, d)
            j = (m - 3) * (1 - d) + (6 - m) * d
            keys = kvx[d, m, pl.ds(first, count)].reshape(256 * count, 128)
            done.append((i, block(q_s[i].reshape(512, 128), keys) * allowed(base + i, base + j)))
        for i, r in done:
            acc[i] += r

    near = t // 2
    far = 1 - near

    def near_pairs(n):
        cross(near, [pair(2 * n), pair(2 * n + 1)], 0, 4)

    w_local.wait()
    other_cols = pl.ds(pl.multiple_of((1 - c) * 128, 128), 128)
    rcopy(w, w3.at[:, :, other_cols], ws_sem.at[0], ws_sem.at[1], sib).wait_recv()
    project_row(4 + t)

    def z_step(k, _):
        def forward(h):
            def one(d, _):
                z = slot(k, d)

                @pl.when(arrives(k, d))
                def _():
                    rcopy(half_of(z, h), half_of(z, h), ag_send.at[z, h], ag_recv.at[z, h], sib).wait_recv()

                    @pl.when(passes_on(k, d))
                    def _():
                        pass_on(k, d, h, z).start()

                return 0

            lax.fori_loop(0, 2, one, 0)

        def spread_step(d, _):
            spread_keys(k - 1, d)
            return 0

        forward(0)

        forward(1)

        @pl.when(k == 1)
        def _():
            row_arrived(4 + t)

        @pl.when(k > 1)
        def _():
            lax.fori_loop(0, 2, spread_step, 0)

        @pl.when(k == 2)
        def _():
            w_out_stage(wa_wait, wy_copy)

        @pl.when(k == 3)
        def _():
            w_out_stage(wy_wait, wb_copy)

        @pl.when(k == 6)
        def _():
            for m in (1, 2, 3):
                wb_wait(m)
            wc.start()

        def project(d, _):
            z = slot(k, d)

            @pl.when(arrives(k, d))
            def _():
                @pl.when(is_row(k, d))
                def _():
                    project_row(z)

                @pl.when(is_cross(k, d))
                def _():
                    project_cross(z, d)

            return 0

        lax.fori_loop(0, 2, project, 0)

        @pl.when(k == 4)
        def _():
            for e in range(4):
                row_sib_wait(4 + e)
            own_images()

        @pl.when((k == 5) | (k == 6))
        def _():
            row_pairs(2 * (k - 5))

        @pl.when(k == 5)
        def _():
            row_pairs(1)

        @pl.when(k == 6)
        def _():
            for e in range(4):
                cross_sib_wait(8 * near + e, near)
            near_pairs(0)

        @pl.when(k == 7)
        def _():
            near_pairs(1)

        return 0

    lax.fori_loop(1, 8, z_step, 0)

    low64 = lax.broadcasted_iota(jnp.int32, (64, 128), 1) < 64
    head = t * 4 + y

    def f_copy(k, m):
        return rcopy(
            fsend.at[(y + k) % 4, (t + m) % 4], fin.at[head], f_send.at[k, m], f_recv.at[k, m], blk_dev(k, m)
        )

    def f_wait(k, m):
        other = ((t + 4 - m) % 4) * 4 + (y + 4 - k) % 4
        rcopy(fsend.at[0, 0], fin.at[other], f_send.at[k, m], f_recv.at[k, m], sib).wait_recv()

    def finish(a):
        i = column(a, far)
        for m in range(4):
            n = acc[i, m * 128:(m + 1) * 128, :]
            r = pltpu.roll(n, 64, 1)
            top = r[:64] / n[:64]
            bottom = n[64:] / r[64:]
            fsend[i, m] = jnp.where(low64, top, bottom).astype(BF)
        k = (i + 4 - y) % 4
        for m in range(1, 4):
            f_copy(k, m).start()

        @pl.when(k > 0)
        def _():
            f_copy(k, 0).start()

    near_pairs(2)
    finish(3)
    for e in range(3):
        cross_sib_wait(8 * far + 1 - far + e, far)
    cross(far, [pair(0), pair(1), pair(2)], 1 - far, 3)

    def last_spread(d, _):
        spread_keys(7, d)
        return 0

    lax.fori_loop(0, 2, last_spread, 0)
    cross(far, [pair(3), pair(4), pair(5)], 1 - far, 3)
    cross_sib_wait(11 * far, far)
    cross(far, [(2, 2), (1, 2), (1, 1)], 3 * far, 1)
    finish(2)
    finish(1)
    cross(far, [(0, 2), (0, 1), (0, 0)], 3 * far, 1)
    finish(0)
    fin[head] = fsend[y, t]
    order_f = [(k, m) for k in range(4) for m in range(4) if k or m]
    rcopy(wo.at[:, c], wo.at[:, 1 - c], wc_sem.at[0], wc_sem.at[1], sib).wait_recv()
    for k, m in order_f:
        f_wait(k, m)

    tops, bottoms = [], []
    for h in range(0, 16, 2):
        f0 = fin[h].astype(F32)
        f1 = fin[h + 1].astype(F32)
        tops.append(jnp.where(low64, f0, pltpu.roll(f1, 64, 1)).astype(BF))
        bottoms.append(jnp.where(low64, pltpu.roll(f0, 64, 1), f1).astype(BF))
    att = jnp.concatenate([jnp.concatenate(tops, axis=1), jnp.concatenate(bottoms, axis=1)], axis=0)
    out[...] = dot(att, wo[...].reshape(1024, 1024)).astype(BF)

    for d in (0, 1):

        @pl.when(passes_on(0, d))
        def _():
            for h in (0, 1):
                pass_on(0, d, h, 12 + d).wait_send()

    w_sib.wait_send()
    for m in (1, 2, 3):
        wa_copy(m).wait_send()
        wy_copy(m).wait_send()
        wb_copy(m).wait_send()
    wc.wait_send()

    def row_sent(z):
        for n in (1, 2, 3):
            row_copy(z, n).wait_send()
            yq_copy(z, n).wait_send()
        row_sib(z).wait_send()

    row_sent(4 + t)

    def sent(i, _):
        k = 1 + i // 2
        d = i % 2
        z = slot(k, d)

        @pl.when(arrives(k, d) & passes_on(k, d))
        def _():
            for h in (0, 1):
                pass_on(k, d, h, z).wait_send()

        @pl.when(is_row(k, d))
        def _():
            row_sent(z)

        @pl.when(is_cross(k, d))
        def _():
            @pl.when(column(y, d) >= 1)
            def _():
                for n in (1, 2, 3):
                    cross_copy(z, d, n).wait_send()

            cross_sib(z, d).wait_send()

        return 0

    lax.fori_loop(0, 14, sent, 0)
    for k, m in order_f:
        f_copy(k, m).wait_send()


def body(tokens, norm_gain, w_qkv, q_gain, k_gain, w_out, covis_mask, capture_rank):
    vm = pl.BlockSpec(memory_space=pltpu.VMEM)
    hbm = pl.BlockSpec(memory_space=pl.ANY)
    dma = pltpu.SemaphoreType.DMA
    result = pl.pallas_call(
        kernel,
        out_shape=jax.ShapeDtypeStruct((128, 1024), BF),
        in_specs=[hbm] * 8,
        out_specs=vm,
        scratch_shapes=[
            pltpu.VMEM((128, 1024), BF),
            pltpu.VMEM((1, 1024), F32),
            pltpu.VMEM((1, 64), F32),
            pltpu.VMEM((1, 64), F32),
            pltpu.SMEM((64, 64), jnp.int32),
            pltpu.SMEM((64,), jnp.int32),
            pltpu.VMEM((12, 128, 1024), BF),
            pltpu.VMEM((3, 1024, 256), BF),
            pltpu.VMEM((256, 256), BF),
            pltpu.VMEM((4, 4, 128, 128), BF),
            pltpu.VMEM((12, 4, 128, 128), BF),
            pltpu.VMEM((4, 4, 128, 128), BF),
            pltpu.VMEM((4, 4, 2, 128, 128), BF),
            pltpu.VMEM((2, 3, 4, 2, 128, 128), BF),
            pltpu.VMEM((4, 512, 128), F32),
            pltpu.VMEM((4, 2, 128, 1024), BF),
            pltpu.VMEM((16, 64, 128), BF),
            pltpu.VMEM((4, 4, 64, 128), BF),
            dma((8,)), dma((2,)), dma((14, 2)), dma((12, 2)),
            dma((4, 4)), dma((4, 4)), dma((12, 4)), dma((12, 4)), dma((12,)), dma((12,)),
            dma((4,)), dma((4,)), dma((4,)), dma((4,)), dma((4,)), dma((4,)), dma((2,)), dma((4, 4)), dma((4, 4)),
        ],
        compiler_params=pltpu.CompilerParams(
            collective_id=0, has_side_effects=True, vmem_limit_bytes=60 * 1024 * 1024
        ),
        cost_estimate=pl.CostEstimate(flops=10_000_000_000, bytes_accessed=4_000_000, transcendentals=15_000_000),
    )(
        tokens[0],
        norm_gain.reshape(1, 1024),
        jnp.transpose(w_qkv, (1, 0, 2)),
        q_gain.reshape(1, 64),
        k_gain.reshape(1, 64),
        w_out,
        covis_mask,
        capture_rank,
    )
    return result[None]


def solution(mesh):
    placed = (
        P("group", "slab", None),
        P(),
        P(None, None, "slab"),
        P(),
        P(),
        P("slab", None),
        P(),
        P(),
    )
    return jax.shard_map(
        body, mesh=mesh, in_specs=placed, out_specs=P("group", "slab", None), check_vma=False
    )
```
